512 devices in a mesh: dom: 128 (over y, z, core), sub: 4 (over x).
Axes of the slice: x: 4, y: 8, z: 8, core: 2. Of those that a mesh axis runs over, the one named last changes fastest.
Arguments:
- fine_nodes: bfloat16 [524288, 512], P(('dom', 'sub')), may hold values from -6 to 6
- edge_tiles: bfloat16 [28672, 128, 128], P(('dom', 'sub')), may hold values from -0.375 to 0.375
- edge_target: int32 [28672], P(('dom', 'sub')), may hold values from 0 to 7
- edge_source: int32 [28672], P(('dom', 'sub')), may hold values from 0 to 11, as said below
- edge_count: int32 [512], P(('dom', 'sub')), may hold values from 14 to 56, as said below
- halo_blocks: int32 [2048], P(('dom', 'sub')), may hold values from 0 to 7
- pool_owner: int32 [4096], P(('dom', 'sub')), may hold values from 0 to 127, as said below
- coarse_tiles: bfloat16 [1024, 128, 128], P(('dom', 'sub')), may hold values from -0.375 to 0.375
- pooled_block_source_index: int32 [1024], P(('dom', 'sub')), may hold values from 1 to 3
- fine_first: bfloat16 [1024, 512], replicated, may hold values from -0.1875 to 0.1875
- fine_bias: float32 [512], replicated, may hold values from -4 to 4
- fine_second: bfloat16 [512, 512], replicated, may hold values from -0.25 to 0.25
- fine_gain: float32 [512], replicated, may hold values from 0.1 to 1.9
- coarse_first: bfloat16 [1024, 512], replicated, may hold values from -0.1875 to 0.1875
- coarse_bias: float32 [512], replicated, may hold values from -4 to 4
- coarse_second: bfloat16 [512, 512], replicated, may hold values from -0.25 to 0.25
- pooled_level_scale_factor: float32 [512], replicated, may hold values from 0.1 to 1.9
Outputs:
- fine_out: bfloat16 [524288, 512], P(('dom', 'sub'))
The draws below stay inside these ranges and needn't reach their ends.
Inputs may be any that keep to these rules, and one draw needn't show every extreme that they name: `edge_source`: entry e of a device's list reads block 8 + e of the source table for e below 4. `edge_count`: some device has all 56 entries live. `pool_owner`: a block's owner lies in the same aligned group of 4 dom indices as the block's device; every device receives exactly one tile of each block index k; one device sends at most 2 blocks to one owner, and some device does so.
All inputs are finite; a program needn't handle non-finite values.
Results may differ from the reference program's by a relative error of at most 0.0051.
Values may be sent and summed in bfloat16 or wider, within the bound.
No kernel may reach another device: no remote copies, remote signals or barrier semaphores. Data moves between devices by JAX's collectives and lax.ppermute only.
A program may use at most 128 MiB of HBM per device.

```python
import jax
import jax.numpy as jnp
from jax import lax

D = 512
BLK = 128
POOL = 8
NB_DEV = 8
HALO = 2
WIN = 4
KC = 2
TILE = 16
E_DEV = 56
CR = 128
NODES = 524288
EDGES = 28672
HALOS = 2048
CEDGES = 1024
N_DOM = 128
N_SUB = 4
DEVICES = 512


def draw_edge_source(key, part):
    key = jax.random.fold_in(key, 12)
    sender_indices = jax.random.randint(key, (DEVICES, E_DEV), 0, NB_DEV + 2 * HALO).astype(jnp.int32)
    leading = NB_DEV + jnp.arange(2 * HALO, dtype=jnp.int32)
    sender_indices = sender_indices.at[:, :2 * HALO].set(jnp.broadcast_to(leading[None, :], (DEVICES, 2 * HALO)))
    return sender_indices.reshape(-1)


def draw_edge_count(key, part):
    key = jax.random.fold_in(key, 11)
    first_key, second_random_key, third_key = jax.random.split(key, 3)
    lowest = max(2 * HALO, E_DEV // 4)
    highest = max(lowest + 1, E_DEV // 2 + 1)
    counts = jax.random.randint(first_key, (DEVICES,), lowest, highest).astype(jnp.int32)
    busy = jax.random.randint(second_random_key, (DEVICES,), 0, 16) == 0
    counts = jnp.where(busy, E_DEV, counts)
    fullest = jax.random.randint(third_key, (), 0, DEVICES)
    return counts.at[fullest].set(E_DEV).astype(jnp.int32)


def draw_pool_owner(key, part):
    key = jax.random.fold_in(key, 13)
    groups = N_DOM // WIN * N_SUB
    orders = jax.vmap(lambda sub_key: jax.random.permutation(sub_key, WIN))(jax.random.split(key, groups))
    orders = orders.reshape(N_DOM // WIN, N_SUB, WIN).astype(jnp.int32)
    inverse = jnp.argsort(orders, axis=-1).astype(jnp.int32)
    dom_index = jnp.arange(N_DOM, dtype=jnp.int32)
    sub_index = jnp.arange(N_SUB, dtype=jnp.int32)
    block_index = jnp.arange(NB_DEV, dtype=jnp.int32)
    window = dom_index // WIN
    position = inverse[window[:, None], sub_index[None, :], (dom_index % WIN)[:, None]]
    member = orders[window[:, None, None], sub_index[None, :, None], (position[:, :, None] + block_index[None, None, :]) % WIN]
    owners = window[:, None, None] * WIN + member
    return owners.reshape(-1).astype(jnp.int32)


def with_ends(values, stream_key, least, top_value):
    extent = values.shape
    place = [jax.random.randint(jax.random.fold_in(stream_key, axis), (), 0, extent[axis]) for axis in range(len(extent))]
    values = values.at[tuple(place)].set(least)
    longest = extent.index(max(extent))
    place[longest] = (place[longest] + 1) % extent[longest]
    return values.at[tuple(place)].set(top_value)


def block_levels(key, shape, cuts, low, top_value):
    level, own = 1.0, jax.random.fold_in(key, 6)
    for dim, shards_of in cuts:
        heights = jnp.exp(jax.random.uniform(jax.random.fold_in(own, dim), (shards_of,), jnp.float32, low / len(cuts), top_value / len(cuts)))
        level = level * jnp.repeat(heights, shape[dim] // shards_of).reshape([-1 if axis == dim else 1 for axis in range(len(shape))])
    return level


def bell_draw(rng, shape, width, limit, cuts=(), kind=jnp.bfloat16):
    level = block_levels(rng, shape, cuts, -0.22, 0.18) if cuts else 1.0
    entries = jax.random.normal(rng, shape, jnp.float32) * width * level
    return jnp.minimum(jnp.maximum(entries, -limit), limit).astype(kind)


def setup_inputs(seed: int = 0) -> dict:
    key_of = jax.random.split(jax.random.key(seed), 18)
    return {
        "fine_nodes": bell_draw(key_of[0], (NODES, D), 1.0, 6.0, ((0, 512),)),
        "edge_tiles": bell_draw(key_of[1], (EDGES, BLK, BLK), (BLK * 2) ** -0.5, 0.375, ((0, 512),)),
        "edge_target": with_ends(jax.random.randint(key_of[2], (EDGES,), 0, NB_DEV), jax.random.fold_in(key_of[2], 1), 0, NB_DEV - 1).astype(jnp.int32),
        "edge_source": draw_edge_source(jax.random.fold_in(key_of[17], 71), 0),
        "edge_count": draw_edge_count(jax.random.fold_in(key_of[17], 71), 0),
        "halo_blocks": with_ends(jax.random.randint(key_of[5], (HALOS,), 0, NB_DEV), jax.random.fold_in(key_of[5], 1), 0, NB_DEV - 1).astype(jnp.int32),
        "pool_owner": draw_pool_owner(jax.random.fold_in(key_of[17], 71), 0),
        "coarse_tiles": bell_draw(key_of[7], (CEDGES, CR, CR), (CR * KC) ** -0.5, 0.375, ((0, 512),)),
        "pooled_block_source_index": with_ends(jax.random.randint(key_of[8], (CEDGES,), 1, N_SUB), jax.random.fold_in(key_of[8], 1), 1, N_SUB - 1).astype(jnp.int32),
        "fine_first": bell_draw(key_of[9], (2 * D, D), (2 * D) ** -0.5, 0.1875),
        "fine_bias": bell_draw(key_of[10], (D,), 1.0, 4.0, (), jnp.float32),
        "fine_second": bell_draw(key_of[11], (D, D), D ** -0.5, 0.25),
        "fine_gain": jnp.clip(1.0 + 0.18 * jax.random.normal(key_of[12], (D,), jnp.float32), 0.1, 1.9),
        "coarse_first": bell_draw(key_of[13], (2 * D, D), (2 * D) ** -0.5, 0.1875),
        "coarse_bias": bell_draw(key_of[14], (D,), 1.0, 4.0, (), jnp.float32),
        "coarse_second": bell_draw(key_of[15], (D, D), D ** -0.5, 0.25),
        "pooled_level_scale_factor": jnp.clip(1.0 + 0.18 * jax.random.normal(key_of[16], (D,), jnp.float32), 0.1, 1.9),
    }


def layer_norm(values, gain_vec):
    row_mean = lax.optimization_barrier(jnp.mean(values, axis=-1, keepdims=True))
    centred = values - row_mean
    variance = lax.optimization_barrier(jnp.mean(centred * centred, axis=-1, keepdims=True))
    return centred * lax.rsqrt(variance + 1e-05) * gain_vec

def node_update(node_rows, messages, weight_in, bias_in, weight_out, gain_vec):
    joined = jnp.concatenate([node_rows, messages], axis=-1)
    hidden_act = jnp.maximum(jnp.dot(joined, weight_in, preferred_element_type=jnp.float32) + bias_in, 0.0)
    hidden_act = hidden_act.astype(jnp.bfloat16)
    projected = jnp.dot(hidden_act, weight_out, preferred_element_type=jnp.float32)
    return layer_norm(projected, gain_vec)

def reference(fine_nodes, edge_tiles, edge_target, edge_source, edge_count, halo_blocks, pool_owner, coarse_tiles, pooled_block_source_index, fine_first, fine_bias, fine_second, fine_gain, coarse_first, coarse_bias, coarse_second, pooled_level_scale_factor):
    blocks = fine_nodes.reshape(DEVICES, NB_DEV, BLK, D)
    sending = halo_blocks.reshape(DEVICES, 2, HALO)
    device_index = jnp.arange(DEVICES, dtype=jnp.int32)
    picked = blocks[device_index[:, None, None], sending]
    empty_rim = jnp.zeros((1, HALO, BLK, D), jnp.bfloat16)
    from_lower = jnp.concatenate([empty_rim, picked[:-1, 1]], axis=0)
    from_upper = jnp.concatenate([picked[1:, 0], empty_rim], axis=0)
    tables = jnp.concatenate([blocks, from_lower, from_upper], axis=1)
    tiles = edge_tiles.reshape(DEVICES, E_DEV, BLK, BLK)
    receiver_indices = edge_target.reshape(DEVICES, E_DEV)
    sources = edge_source.reshape(DEVICES, E_DEV)

    def aggregate(item):
        sender_index_matrix, tile_set, target_row, source_row, count = item
        gathered = sender_index_matrix[source_row].astype(jnp.float32)
        products = jnp.einsum('ers,esd->erd', tile_set.astype(jnp.float32), gathered)
        live_mask = (jnp.arange(E_DEV, dtype=jnp.int32) < count).astype(jnp.float32)
        onehot = (target_row[:, None] == jnp.arange(NB_DEV, dtype=jnp.int32)[None, :]).astype(jnp.float32)
        onehot = onehot * live_mask[:, None]
        return jnp.einsum('eb,erd->brd', onehot, products, precision=lax.Precision.HIGHEST)
    messages = lax.map(aggregate, (tables, tiles, receiver_indices, sources, edge_count))
    messages = messages.astype(jnp.bfloat16).reshape(NODES, D)
    fine_delta = node_update(fine_nodes, messages, fine_first, fine_bias, fine_second, fine_gain)
    pooled = lax.optimization_barrier(jnp.mean(fine_nodes.astype(jnp.float32).reshape(DEVICES, NB_DEV, TILE, POOL, D), axis=3))
    pooled = pooled.astype(jnp.bfloat16)
    owners = pool_owner.reshape(DEVICES, NB_DEV)
    owner_device = owners * N_SUB + (device_index % N_SUB)[:, None]
    block_index = jnp.broadcast_to(jnp.arange(NB_DEV, dtype=jnp.int32)[None, :], (DEVICES, NB_DEV))
    coarse = jnp.zeros((DEVICES, NB_DEV, TILE, D), jnp.bfloat16).at[owner_device, block_index].set(pooled)
    pooled_level_vectors = coarse.reshape(DEVICES, CR, D)
    coarse_node_collection = coarse_tiles.reshape(DEVICES, KC, CR, CR)
    source_sub = ((device_index % N_SUB)[:, None] + pooled_block_source_index.reshape(DEVICES, KC)) % N_SUB
    coarse_from = (device_index // N_SUB)[:, None] * N_SUB + source_sub
    coarse_lookup_rows = pooled_level_vectors[coarse_from]
    coarse_message_rows = jnp.einsum('ejgz,ejzi->egi', coarse_node_collection.astype(jnp.float32), coarse_lookup_rows.astype(jnp.float32), precision=lax.Precision.HIGHEST)
    coarse_message_rows = coarse_message_rows.astype(jnp.bfloat16).reshape(DEVICES * CR, D)
    coarse_delta = node_update(pooled_level_vectors.reshape(DEVICES * CR, D), coarse_message_rows, coarse_first, coarse_bias, coarse_second, pooled_level_scale_factor)
    coarse_delta = coarse_delta.astype(jnp.bfloat16).reshape(DEVICES, NB_DEV, TILE, D)
    returned = coarse_delta[owner_device, block_index]
    unpooled = jnp.repeat(returned, POOL, axis=2).reshape(NODES, D)
    fine_out = fine_nodes.astype(jnp.float32) + fine_delta + unpooled.astype(jnp.float32)
    return fine_out.astype(jnp.bfloat16)
```

```python
import functools

import jax
import jax.numpy as jnp
from jax import lax
from jax.experimental import pallas as pl
from jax.experimental.pallas import tpu as pltpu
from jax.sharding import Mesh
from jax.sharding import PartitionSpec as P

POOL = 8
WIN = 4
GROUP = 4
F32 = jnp.float32
BF16 = jnp.bfloat16

VMEM_SPEC = pl.BlockSpec(memory_space=pltpu.VMEM)
SMEM_SPEC = pl.BlockSpec(memory_space=pltpu.SMEM)
ANY_SPEC = pl.BlockSpec(memory_space=pl.ANY)


def owner_slots(owner_ref, count_ref, block_count):
    for d in range(WIN):
        count_ref[d] = 0
    slots = []
    for k in range(block_count):
        d = owner_ref[k] & (WIN - 1)
        r = count_ref[d]
        count_ref[d] = r + 1
        slots.append((d, r))
    return slots


def pack_kernel(owner_ref, halo_ref, nodes_ref, send_ref, lower_ref, upper_ref, count_ref, index_ref):
    blocks, rows, width = nodes_ref.shape
    tile = rows // POOL
    lanes = send_ref.shape[-1]
    groups = width // lanes
    subs = send_ref.shape[0] // WIN
    halo = halo_ref.shape[0] // 2
    for h in range(halo):
        lower_ref[h] = nodes_ref[halo_ref[h]]
        upper_ref[h] = nodes_ref[halo_ref[halo + h]]
    row = lax.broadcasted_iota(jnp.int32, (tile, rows), 0)
    col = lax.broadcasted_iota(jnp.int32, (tile, rows), 1)
    average = jnp.where(col // POOL == row, 1.0 / POOL, 0.0).astype(BF16)
    for k, (d, r) in enumerate(owner_slots(owner_ref, count_ref, blocks)):
        index_ref[d * 2 + r] = k
        pooled = jnp.dot(average, nodes_ref[k], preferred_element_type=F32).astype(BF16)
        for s in range(subs):
            for c in range(groups):
                send_ref[d * subs + s, c * 2 + r] = pooled[:, c * lanes : (c + 1) * lanes]
    lane = lax.broadcasted_iota(jnp.int32, (tile, lanes), 1)
    for d in range(WIN):
        tag = jnp.where((lane // tile) % 2 == 0, index_ref[2 * d], index_ref[2 * d + 1])
        tag = tag.astype(F32).astype(BF16)
        for s in range(subs):
            send_ref[d * subs + s, groups * 2] = tag


def pack(pool_owner, halo_blocks, blocks, subs):
    count, rows, width = blocks.shape
    tile = rows // POOL
    halo = halo_blocks.shape[0] // 2
    lanes = 128
    return pl.pallas_call(
        pack_kernel,
        name="pack",
        out_shape=(
            jax.ShapeDtypeStruct((WIN * subs, 2 * (width // lanes) + 1, tile, lanes), BF16),
            jax.ShapeDtypeStruct((halo, rows, width), BF16),
            jax.ShapeDtypeStruct((halo, rows, width), BF16),
        ),
        in_specs=[SMEM_SPEC, SMEM_SPEC, VMEM_SPEC],
        out_specs=(VMEM_SPEC,) * 3,
        scratch_shapes=[pltpu.SMEM((WIN,), jnp.int32), pltpu.SMEM((2 * WIN,), jnp.int32)],
        compiler_params=pltpu.CompilerParams(vmem_limit_bytes=16 << 20),
        cost_estimate=pl.CostEstimate(flops=1 << 27, bytes_accessed=3 << 20, transcendentals=0),
    )(pool_owner, halo_blocks, blocks)


def normalised(values, gain):
    row_mean = jnp.mean(values, axis=-1, keepdims=True)
    centred = values - row_mean
    variance = jnp.mean(centred * centred, axis=-1, keepdims=True)
    return centred * lax.rsqrt(variance + 1e-05) * gain


def network(nodes, messages, first_ref, bias_ref, second_ref, gain_ref):
    width = nodes.shape[1]
    hidden = jnp.dot(nodes, first_ref[:width], preferred_element_type=F32)
    hidden += jnp.dot(messages, first_ref[width:], preferred_element_type=F32)
    hidden = jnp.maximum(hidden + bias_ref[...], 0.0).astype(BF16)
    projected = jnp.dot(hidden, second_ref[...], preferred_element_type=F32)
    return normalised(projected, gain_ref[...])


def coarse_kernel(sub_ref, arrived_ref, tiles_ref, first_ref, bias_ref, second_ref, gain_ref, reply_ref):
    senders, pieces, tile, lanes = arrived_ref.shape
    groups = pieces // 2
    subs = senders // WIN
    rows = tiles_ref.shape[1]
    row = lax.broadcasted_iota(jnp.int32, (rows, rows), 0)
    col = lax.broadcasted_iota(jnp.int32, (rows, rows), 1)
    same_row = row % tile == col % tile

    def arrived_rows(s):
        return jnp.concatenate(
            [
                jnp.concatenate([arrived_ref[m * subs + s, c * 2 + r] for c in range(groups)], axis=1)
                for m in range(WIN)
                for r in range(2)
            ],
            axis=0,
        )

    def placing(s):
        tags = jnp.zeros((8, lanes), F32)
        lane = lax.broadcasted_iota(jnp.int32, (8, lanes), 1)
        for m in range(WIN):
            tag = arrived_ref[m * subs + s, groups * 2].astype(F32)[:8]
            tags = jnp.where(lane // (2 * tile) == m, tag, tags)
        return jnp.where(same_row & (row // tile == tags[:1].astype(jnp.int32)), 1.0, 0.0)

    own = sub_ref[0]
    own_rows = arrived_rows(own)
    own_back = placing(own).T.astype(BF16)
    weights, sources = [], []
    for e in range(tiles_ref.shape[0]):
        s = sub_ref[1 + e]
        sources.append(arrived_rows(s))
        by_col = jnp.dot(tiles_ref[e], placing(s).astype(BF16), preferred_element_type=F32)
        weights.append(by_col.astype(BF16))
    by_col = jnp.concatenate(weights, axis=1)
    by_both = jnp.dot(own_back, by_col, preferred_element_type=F32).astype(BF16)
    messages = jnp.dot(by_both, jnp.concatenate(sources, axis=0), preferred_element_type=F32)
    delta = network(own_rows, messages.astype(BF16), first_ref, bias_ref, second_ref, gain_ref)
    delta = delta.astype(BF16)
    for m in range(WIN):
        for r in range(2):
            at = (m * 2 + r) * tile
            reply_ref[m, r] = delta[at : at + tile]


def coarse_update(sub_index, arrived, tiles, first, bias, second, gain):
    width = second.shape[0]
    tile = arrived.shape[2]
    return pl.pallas_call(
        coarse_kernel,
        name="coarse",
        out_shape=jax.ShapeDtypeStruct((WIN, 2, tile, width), BF16),
        in_specs=[SMEM_SPEC] + [VMEM_SPEC] * 6,
        out_specs=VMEM_SPEC,
        compiler_params=pltpu.CompilerParams(vmem_limit_bytes=16 << 20),
        cost_estimate=pl.CostEstimate(flops=1 << 29, bytes_accessed=3 << 20, transcendentals=0),
    )(sub_index, arrived, tiles, first, bias, second, gain)


def message_kernel(
    target_ref, source_ref, count_ref, nodes_ref, lower_ref, upper_ref, edges_ref, out_ref,
    table, tiles, total, order_e, order_s, place, sems,
):
    blocks, rows, width = nodes_ref.shape
    entries = edges_ref.shape[0]
    halo = lower_ref.shape[0]
    copies = [
        pltpu.make_async_copy(nodes_ref, table.at[pl.ds(0, blocks)], sems.at[0]),
        pltpu.make_async_copy(edges_ref, tiles.at[pl.ds(0, entries)], sems.at[1]),
        pltpu.make_async_copy(lower_ref, table.at[pl.ds(blocks, halo)], sems.at[2]),
        pltpu.make_async_copy(upper_ref, table.at[pl.ds(blocks + halo, halo)], sems.at[3]),
    ]
    for copy in copies:
        copy.start()
    tiles[entries] = jnp.zeros((rows, rows), BF16)
    live = count_ref[0]

    for b in range(blocks):
        place[b] = 0

    @pl.loop(0, order_e.shape[0])
    def _(i):
        order_e[i] = entries
        order_s[i] = 0

    @pl.loop(0, live)
    def _(e):
        b = target_ref[e]
        place[b] = place[b] + 1

    begins, at = [], 0
    for b in range(blocks):
        steps = (place[b] + (GROUP - 1)) // GROUP
        begins.append((at, steps))
        place[b] = at * GROUP
        at = at + steps

    @pl.loop(0, live)
    def _(e):
        b = target_ref[e]
        at = place[b]
        place[b] = at + 1
        order_e[at] = e
        order_s[at] = source_ref[e]

    for copy in copies:
        copy.wait()
    for b, (begin, steps) in enumerate(begins):
        total[...] = jnp.zeros_like(total)

        @pl.loop(0, steps)
        def _(i):
            at = (begin + i) * GROUP
            left = jnp.concatenate([tiles[order_e[at + g]] for g in range(GROUP)], axis=1)
            right = jnp.concatenate([table[order_s[at + g]] for g in range(GROUP)], axis=0)
            total[...] += jnp.dot(left, right, preferred_element_type=F32)

        out_ref[b] = total[...].astype(BF16)


def block_messages(target, source, count, blocks, lower, upper, edges):
    entries, rows, _ = edges.shape
    block_count, _, width = blocks.shape
    halo = lower.shape[0]
    slots = (entries // GROUP + block_count) * GROUP
    return pl.pallas_call(
        message_kernel,
        name="messages",
        out_shape=jax.ShapeDtypeStruct(blocks.shape, BF16),
        in_specs=[SMEM_SPEC] * 3 + [ANY_SPEC] * 4,
        out_specs=VMEM_SPEC,
        scratch_shapes=[
            pltpu.VMEM((block_count + 2 * halo, rows, width), BF16),
            pltpu.VMEM((entries + 1, rows, rows), BF16),
            pltpu.VMEM((rows, width), F32),
            pltpu.SMEM((slots,), jnp.int32),
            pltpu.SMEM((slots,), jnp.int32),
            pltpu.SMEM((block_count,), jnp.int32),
            pltpu.SemaphoreType.DMA((4,)),
        ],
        compiler_params=pltpu.CompilerParams(vmem_limit_bytes=16 << 20),
        cost_estimate=pl.CostEstimate(flops=1 << 32, bytes_accessed=6 << 20, transcendentals=0),
    )(target, source, count, blocks, lower, upper, edges)


def fine_kernel(nodes_ref, messages_ref, first_ref, bias_ref, second_ref, gain_ref, out_ref):
    step = 256

    @pl.loop(0, nodes_ref.shape[0] // step)
    def _(i):
        at = pl.ds(pl.multiple_of(i * step, step), step)
        nodes = nodes_ref[at]
        delta = network(nodes, messages_ref[at], first_ref, bias_ref, second_ref, gain_ref)
        out_ref[at] = nodes.astype(F32) + delta


def fine_update(nodes, messages, first, bias, second, gain):
    return pl.pallas_call(
        fine_kernel,
        name="fine",
        out_shape=jax.ShapeDtypeStruct(nodes.shape, F32),
        in_specs=[VMEM_SPEC] * 6,
        out_specs=VMEM_SPEC,
        compiler_params=pltpu.CompilerParams(vmem_limit_bytes=16 << 20),
        cost_estimate=pl.CostEstimate(flops=1 << 31, bytes_accessed=6 << 20, transcendentals=0),
    )(nodes, messages, first, bias, second, gain)


def finish_kernel(owner_ref, partial_ref, reply_ref, out_ref, count_ref):
    blocks = owner_ref.shape[0]
    rows = partial_ref.shape[0] // blocks
    tile = rows // POOL
    row = lax.broadcasted_iota(jnp.int32, (rows, tile), 0)
    col = lax.broadcasted_iota(jnp.int32, (rows, tile), 1)
    spread = jnp.where(row // POOL == col, 1.0, 0.0).astype(BF16)
    for k, (d, r) in enumerate(owner_slots(owner_ref, count_ref, blocks)):
        back = jnp.dot(spread, reply_ref[d, r], preferred_element_type=F32)
        at = pl.ds(k * rows, rows)
        out_ref[at] = (partial_ref[at] + back).astype(BF16)


def finish(pool_owner, partial, reply):
    return pl.pallas_call(
        finish_kernel,
        name="finish",
        out_shape=jax.ShapeDtypeStruct(partial.shape, BF16),
        in_specs=[SMEM_SPEC, VMEM_SPEC, VMEM_SPEC],
        out_specs=VMEM_SPEC,
        scratch_shapes=[pltpu.SMEM((WIN,), jnp.int32)],
        compiler_params=pltpu.CompilerParams(vmem_limit_bytes=16 << 20),
        cost_estimate=pl.CostEstimate(flops=1 << 25, bytes_accessed=4 << 20, transcendentals=0),
    )(pool_owner, partial, reply)


def per_device(
    fine_nodes,
    edge_tiles,
    edge_target,
    edge_source,
    edge_count,
    halo_blocks,
    pool_owner,
    coarse_tiles,
    pooled_block_source_index,
    fine_first,
    fine_bias,
    fine_second,
    fine_gain,
    coarse_first,
    coarse_bias,
    coarse_second,
    pooled_level_scale_factor,
):
    block_count = pool_owner.shape[0]
    rows = edge_tiles.shape[1]
    width = fine_nodes.shape[1]
    subs = lax.axis_size("sub")
    everyone = ("win", "mem", "sub")
    devices = lax.axis_size(everyone)
    blocks = fine_nodes.reshape(block_count, rows, width)

    send, lower, upper = pack(pool_owner, halo_blocks, blocks, subs)
    arrived = lax.all_to_all(send, ("mem", "sub"), 0, 0, tiled=True)
    from_lower = lax.ppermute(upper, everyone, [(i, i + 1) for i in range(devices - 1)])
    from_upper = lax.ppermute(lower, everyone, [(i + 1, i) for i in range(devices - 1)])
    messages = block_messages(
        edge_target, edge_source, edge_count, blocks, from_lower, from_upper, edge_tiles
    )

    own_sub = lax.axis_index("sub").astype(jnp.int32)
    sub_index = jnp.concatenate([own_sub[None], (own_sub + pooled_block_source_index) % subs])
    reply = coarse_update(
        sub_index,
        arrived,
        coarse_tiles,
        coarse_first,
        coarse_bias[None],
        coarse_second,
        pooled_level_scale_factor[None],
    )
    returned = lax.all_to_all(reply, "mem", 0, 0, tiled=True)
    partial = fine_update(
        fine_nodes,
        messages.reshape(fine_nodes.shape),
        fine_first,
        fine_bias[None],
        fine_second,
        fine_gain[None],
    )
    return finish(pool_owner, partial, returned)


def solution(mesh):
    dom, sub = mesh.devices.shape
    split = Mesh(mesh.devices.reshape(dom // WIN, WIN, sub), ("win", "mem", "sub"))
    every = ("win", "mem", "sub")
    placed = (
        P(every, None),
        P(every, None, None),
        P(every),
        P(every),
        P(every),
        P(every),
        P(every),
        P(every, None, None),
        P(every),
        P(),
        P(),
        P(),
        P(),
        P(),
        P(),
        P(),
        P(),
    )
    return jax.shard_map(
        per_device, mesh=split, in_specs=placed, out_specs=P(every, None), check_vma=False
    )
```

```python
import jax
import jax.numpy as jnp
from jax import lax
from jax.experimental import pallas as pl
from jax.experimental.pallas import tpu as pltpu
from jax.sharding import Mesh
from jax.sharding import PartitionSpec as P

POOL = 8
WIN = 4
ROW = 64
DEPTH = 2
SIDE = 2
F32 = jnp.float32
BF16 = jnp.bfloat16

VMEM_SPEC = pl.BlockSpec(memory_space=pltpu.VMEM)
SMEM_SPEC = pl.BlockSpec(memory_space=pltpu.SMEM)
HBM_SPEC = pl.BlockSpec(memory_space=pltpu.HBM)
ANY_SPEC = pl.BlockSpec(memory_space=pl.ANY)


def room_for(*arrays):
    taken = sum(array.size * array.dtype.itemsize for array in arrays)
    return pltpu.CompilerParams(vmem_limit_bytes=(64 << 20) - taken)


PARAMS = room_for()


def started(pairs, sems):
    copies = [pltpu.make_async_copy(src, dst, sems.at[i]) for i, (src, dst) in enumerate(pairs)]
    for copy in copies:
        copy.start()
    return copies


def owner_slots(owner_ref, count_ref, block_count):
    for d in range(WIN):
        count_ref[d] = 0
    slots = []
    for k in range(block_count):
        d = owner_ref[k] & (WIN - 1)
        r = count_ref[d]
        count_ref[d] = r + 1
        slots.append((d, r))
    return slots


def pack_kernel(
    owner_hbm, halo_hbm, nodes_hbm, send_hbm, lower_hbm, upper_hbm,
    owner_ref, halo_ref, nodes_ref, send_ref, count_ref, index_ref, int_sems, node_sems, halo_sems, send_sems,
):
    blocks, rows, width = nodes_ref.shape
    tile = rows // POOL
    lanes = send_ref.shape[-1]
    groups = width // lanes
    subs = send_hbm.shape[0] // WIN
    halo = halo_ref.shape[0] // 2
    ints = started([(owner_hbm, owner_ref), (halo_hbm, halo_ref)], int_sems)
    loads = started([(nodes_hbm.at[k], nodes_ref.at[k]) for k in range(blocks)], node_sems)
    for copy in ints:
        copy.wait()
    row = lax.broadcasted_iota(jnp.int32, (tile, rows), 0)
    col = lax.broadcasted_iota(jnp.int32, (tile, rows), 1)
    average = jnp.where(col // POOL == row, 1.0 / POOL, 0.0).astype(BF16)
    slots = owner_slots(owner_ref, count_ref, blocks)
    for k, (d, r) in enumerate(slots):
        index_ref[d * 2 + r] = k
    lane = lax.broadcasted_iota(jnp.int32, (tile, lanes), 1)
    for d in range(WIN):
        tag = jnp.where((lane // tile) % 2 == 0, index_ref[2 * d], index_ref[2 * d + 1])
        send_ref[d, groups * 2] = tag.astype(F32).astype(BF16)
    for k, (d, r) in enumerate(slots):
        loads[k].wait()
        pooled = jnp.dot(average, nodes_ref[k], preferred_element_type=F32).astype(BF16)
        for c in range(groups):
            send_ref[d, c * 2 + r] = pooled[:, c * lanes : (c + 1) * lanes]
    halos = started(
        [(nodes_ref.at[halo_ref[h]], lower_hbm.at[h]) for h in range(halo)]
        + [(nodes_ref.at[halo_ref[halo + h]], upper_hbm.at[h]) for h in range(halo)],
        halo_sems,
    )
    sends = started(
        [(send_ref.at[d], send_hbm.at[d * subs + s]) for d in range(WIN) for s in range(subs)], send_sems
    )
    for copy in halos + sends:
        copy.wait()


def pack(pool_owner, halo_blocks, blocks, subs):
    count, rows, width = blocks.shape
    tile = rows // POOL
    halos = halo_blocks.shape[0]
    lanes = 128
    pieces = 2 * (width // lanes) + 1
    return pl.pallas_call(
        pack_kernel,
        name="pack",
        out_shape=(
            jax.ShapeDtypeStruct((WIN * subs, pieces, tile, lanes), BF16),
            jax.ShapeDtypeStruct((halos // 2, rows, width), BF16),
            jax.ShapeDtypeStruct((halos // 2, rows, width), BF16),
        ),
        in_specs=[HBM_SPEC] * 3,
        out_specs=(ANY_SPEC,) * 3,
        scratch_shapes=[
            pltpu.SMEM((count,), jnp.int32),
            pltpu.SMEM((halos,), jnp.int32),
            pltpu.VMEM(blocks.shape, BF16),
            pltpu.VMEM((WIN, pieces, tile, lanes), BF16),
            pltpu.SMEM((WIN,), jnp.int32),
            pltpu.SMEM((2 * WIN,), jnp.int32),
            pltpu.SemaphoreType.DMA((2,)),
            pltpu.SemaphoreType.DMA((count,)),
            pltpu.SemaphoreType.DMA((halos,)),
            pltpu.SemaphoreType.DMA((WIN * subs,)),
        ],
        compiler_params=PARAMS,
        cost_estimate=pl.CostEstimate(flops=1 << 27, bytes_accessed=3 << 20, transcendentals=0),
    )(pool_owner, halo_blocks, blocks)


def normalised(values, gain):
    row_mean = jnp.mean(values, axis=-1, keepdims=True)
    centred = values - row_mean
    variance = jnp.mean(centred * centred, axis=-1, keepdims=True)
    return centred * lax.rsqrt(variance + 1e-05) * gain


def network(nodes, messages, first_ref, bias_ref, second_ref, gain_ref):
    width = nodes.shape[1]
    hidden = jnp.dot(nodes, first_ref[:width], preferred_element_type=F32)
    hidden += jnp.dot(messages, first_ref[width:], preferred_element_type=F32)
    hidden = jnp.maximum(hidden + bias_ref[...], 0.0).astype(BF16)
    projected = jnp.dot(hidden, second_ref[...], preferred_element_type=F32)
    return normalised(projected, gain_ref[...])


def coarse_kernel(
    sub_ref, offset_hbm, arrived_hbm, tiles_hbm, first_hbm, bias_hbm, second_hbm, gain_hbm, after_hbm, reply_hbm,
    offset_ref, arrived_ref, tiles_ref, first_ref, bias_ref, second_ref, gain_ref, reply_ref, sems,
):
    senders, pieces, tile, lanes = arrived_ref.shape
    groups = pieces // 2
    subs = senders // WIN
    entries, rows, _ = tiles_ref.shape
    loads = started(
        [
            (offset_hbm, offset_ref),
            (arrived_hbm, arrived_ref),
            (tiles_hbm, tiles_ref),
            (first_hbm, first_ref),
            (bias_hbm, bias_ref.at[0]),
            (second_hbm, second_ref),
            (gain_hbm, gain_ref.at[0]),
        ],
        sems,
    )
    row = lax.broadcasted_iota(jnp.int32, (rows, rows), 0)
    col = lax.broadcasted_iota(jnp.int32, (rows, rows), 1)
    same_row = row % tile == col % tile

    def arrived_rows(s):
        return jnp.concatenate(
            [
                jnp.concatenate([arrived_ref[m * subs + s, c * 2 + r] for c in range(groups)], axis=1)
                for m in range(WIN)
                for r in range(2)
            ],
            axis=0,
        )

    def placing(s):
        tags = jnp.zeros((8, lanes), F32)
        lane = lax.broadcasted_iota(jnp.int32, (8, lanes), 1)
        for m in range(WIN):
            tag = arrived_ref[m * subs + s, groups * 2].astype(F32)[:8]
            tags = jnp.where(lane // (2 * tile) == m, tag, tags)
        return jnp.where(same_row & (row // tile == tags[:1].astype(jnp.int32)), 1.0, 0.0)

    own = sub_ref[0]
    for copy in loads[:3]:
        copy.wait()
    own_rows = arrived_rows(own)
    own_back = placing(own).T.astype(BF16)
    weights, sources = [], []
    for e in range(entries):
        s = lax.rem(own + offset_ref[e], subs)
        sources.append(arrived_rows(s))
        by_col = jnp.dot(tiles_ref[e], placing(s).astype(BF16), preferred_element_type=F32)
        weights.append(by_col.astype(BF16))
    by_col = jnp.concatenate(weights, axis=1)
    by_both = jnp.dot(own_back, by_col, preferred_element_type=F32).astype(BF16)
    messages = jnp.dot(by_both, jnp.concatenate(sources, axis=0), preferred_element_type=F32)
    for copy in loads[3:]:
        copy.wait()
    delta = network(own_rows, messages.astype(BF16), first_ref, bias_ref, second_ref, gain_ref)
    delta = delta.astype(BF16)
    for m in range(WIN):
        for r in range(2):
            at = (m * 2 + r) * tile
            reply_ref[m, r] = delta[at : at + tile]
    out = pltpu.make_async_copy(reply_ref, reply_hbm, sems.at[0])
    out.start()
    out.wait()


def coarse_update(own_sub, offsets, arrived, tiles, first, bias, second, gain, after):
    width = second.shape[0]
    tile = arrived.shape[2]
    reply = jax.ShapeDtypeStruct((WIN, 2, tile, width), BF16)
    return pl.pallas_call(
        coarse_kernel,
        name="coarse",
        out_shape=reply,
        in_specs=[SMEM_SPEC, HBM_SPEC, ANY_SPEC] + [HBM_SPEC] * 5 + [ANY_SPEC],
        out_specs=ANY_SPEC,
        scratch_shapes=[
            pltpu.SMEM(offsets.shape, jnp.int32),
            pltpu.VMEM(arrived.shape, BF16),
            pltpu.VMEM(tiles.shape, BF16),
            pltpu.VMEM(first.shape, BF16),
            pltpu.VMEM((1, width), F32),
            pltpu.VMEM(second.shape, BF16),
            pltpu.VMEM((1, width), F32),
            pltpu.VMEM(reply.shape, BF16),
            pltpu.SemaphoreType.DMA((7,)),
        ],
        compiler_params=room_for(arrived),
        cost_estimate=pl.CostEstimate(flops=1 << 29, bytes_accessed=3 << 20, transcendentals=0),
    )(own_sub, offsets, arrived, tiles, first, bias, second, gain, after)


def add_messages(
    target_ref, source_ref, live, table, tiles, total, order, place, loads
):
    blocks = total.shape[0]
    entries = target_ref.shape[0]
    slots = order.shape[0]
    for b in range(blocks + 1):
        place[b] = 0
    for i in range(slots):
        order[i] = entries
    bins = []
    for e in range(entries):
        b = jnp.where(e < live, target_ref[e], blocks)
        place[b] = place[b] + 1
        bins.append(b)
    at = 0
    for b in range(blocks):
        steps = (place[b] + (DEPTH - 1)) // DEPTH
        place[b] = at * DEPTH
        at = at + steps
    place[blocks] = slots - entries
    used = at
    for e in range(entries):
        at = place[bins[e]]
        place[bins[e]] = at + 1
        order[at] = e + (source_ref[e] << 8) + (bins[e] << 16)
    for copy in loads:
        copy.wait()

    @pl.loop(0, (used + (SIDE - 1)) // SIDE)
    def _(i):
        products = []
        for u in range(SIDE):
            codes = [order[(i * SIDE + u) * DEPTH + g] for g in range(DEPTH)]
            left = jnp.concatenate([tiles[code & 255] for code in codes], axis=1)
            right = jnp.concatenate([table[(code >> 8) & 255] for code in codes], axis=0)
            product = jnp.dot(left, right, preferred_element_type=F32)
            products.append((codes[0] >> 16, product))
        for b, product in products:
            total[b] += product


def order_slots(entries, blocks):
    groups = entries // DEPTH + blocks
    return (groups + SIDE - 1) // SIDE * SIDE * DEPTH + entries


def fine_body(
    target_hbm, source_hbm, count_ref, lower_hbm, upper_hbm, edges_hbm, nodes_hbm,
    first_hbm, bias_hbm, second_hbm, gain_hbm, out_hbm,
    target_ref, source_ref, table, tiles, total, order, place,
    first_ref, bias_ref, second_ref, gain_ref, out_ref, sems, out_sems,
):
    entries = edges_hbm.shape[0]
    halo = lower_hbm.shape[0]
    blocks, rows, width = total.shape
    loads = started(
        [
            (target_hbm, target_ref),
            (source_hbm, source_ref),
            (edges_hbm, tiles.at[pl.ds(0, entries)]),
            (nodes_hbm, table.at[pl.ds(0, blocks)]),
            (lower_hbm, table.at[pl.ds(blocks, halo)]),
            (upper_hbm, table.at[pl.ds(blocks + halo, halo)]),
            (first_hbm, first_ref),
            (second_hbm, second_ref),
            (bias_hbm, bias_ref.at[0]),
            (gain_hbm, gain_ref.at[0]),
        ],
        sems,
    )
    tiles[entries] = jnp.zeros(tiles.shape[1:], BF16)
    total[...] = jnp.zeros_like(total)
    for copy in loads[:2]:
        copy.wait()
    add_messages(target_ref, source_ref, count_ref[0], table, tiles, total, order, place, loads[2:6])
    for copy in loads[6:]:
        copy.wait()
    outs = []
    for i in range(blocks // 2):
        at = pl.ds(2 * i, 2)
        nodes = table[2 * i : 2 * i + 2].reshape(2 * rows, width)
        messages = total[2 * i : 2 * i + 2].reshape(2 * rows, width).astype(BF16)
        delta = network(nodes, messages, first_ref, bias_ref, second_ref, gain_ref)
        out_ref[2 * i : 2 * i + 2] = (nodes.astype(F32) + delta).reshape(2, rows, width)
        outs += started([(out_ref.at[at], out_hbm.at[at])], out_sems.at[pl.ds(i, 1)])
    for out in outs:
        out.wait()


def fine_kernel(late_ref, *refs):
    @pl.when(late_ref[0] == 0)
    def _():
        fine_body(*refs)


def late_kernel(late_ref, done_hbm, after_hbm, *refs):
    @pl.when(late_ref[0] == 1)
    def _():
        fine_body(*refs)


def fine_update(late, entries, lower, upper, edges, nodes, first, bias, second, gain, done=None, after=None):
    entry_count, rows, _ = edges.shape
    block_count, _, width = nodes.shape
    halo = lower.shape[0]
    target, source, count = entries
    held = [] if done is None else [done, after]
    return pl.pallas_call(
        fine_kernel if done is None else late_kernel,
        name="fine" if done is None else "late",
        out_shape=jax.ShapeDtypeStruct(nodes.shape, F32),
        in_specs=[SMEM_SPEC]
        + [ANY_SPEC] * len(held)
        + [HBM_SPEC, HBM_SPEC, SMEM_SPEC, ANY_SPEC, ANY_SPEC]
        + [HBM_SPEC] * 6,
        out_specs=ANY_SPEC,
        input_output_aliases={1: 0} if held else {},
        scratch_shapes=[
            pltpu.SMEM((entry_count,), jnp.int32),
            pltpu.SMEM((entry_count,), jnp.int32),
            pltpu.VMEM((block_count + 2 * halo, rows, width), BF16),
            pltpu.VMEM((entry_count + 1, rows, rows), BF16),
            pltpu.VMEM(nodes.shape, F32),
            pltpu.SMEM((order_slots(entry_count, block_count),), jnp.int32),
            pltpu.SMEM((block_count + 1,), jnp.int32),
            pltpu.VMEM(first.shape, BF16),
            pltpu.VMEM((1, width), F32),
            pltpu.VMEM(second.shape, BF16),
            pltpu.VMEM((1, width), F32),
            pltpu.VMEM(nodes.shape, F32),
            pltpu.SemaphoreType.DMA((10,)),
            pltpu.SemaphoreType.DMA((block_count // 2,)),
        ],
        compiler_params=PARAMS,
        cost_estimate=pl.CostEstimate(
            flops=1 << (20 if held else 37), bytes_accessed=1 << 20, transcendentals=0
        ),
    )(late, *held, target, source, count, lower, upper, edges, nodes, first, bias, second, gain)


def finish_kernel(
    owner_hbm, partial_hbm, reply_hbm, out_hbm,
    owner_ref, partial_ref, reply_ref, out_ref, count_ref, sems, in_sems, out_sems,
):
    blocks, rows, _ = partial_ref.shape
    tile = rows // POOL
    loads = started([(owner_hbm, owner_ref), (reply_hbm, reply_ref)], sems)
    pairs = [pl.ds(2 * i, 2) for i in range(blocks // 2)]
    parts = started([(partial_hbm.at[at], partial_ref.at[at]) for at in pairs], in_sems)
    row = lax.broadcasted_iota(jnp.int32, (rows, tile), 0)
    col = lax.broadcasted_iota(jnp.int32, (rows, tile), 1)
    spread = jnp.where(row // POOL == col, 1.0, 0.0).astype(BF16)
    for copy in loads:
        copy.wait()
    slots = owner_slots(owner_ref, count_ref, blocks)
    outs = []
    for i, at in enumerate(pairs):
        parts[i].wait()
        for k in (2 * i, 2 * i + 1):
            d, r = slots[k]
            back = jnp.dot(spread, reply_ref[d, r], preferred_element_type=F32)
            out_ref[k] = (partial_ref[k] + back).astype(BF16)
        outs += started([(out_ref.at[at], out_hbm.at[at])], out_sems.at[pl.ds(i, 1)])
    for out in outs:
        out.wait()


def finish(pool_owner, partial, reply):
    blocks = pool_owner.shape[0]
    return pl.pallas_call(
        finish_kernel,
        name="finish",
        out_shape=jax.ShapeDtypeStruct(partial.shape, BF16),
        in_specs=[HBM_SPEC, ANY_SPEC, ANY_SPEC],
        out_specs=ANY_SPEC,
        scratch_shapes=[
            pltpu.SMEM((blocks,), jnp.int32),
            pltpu.VMEM(partial.shape, F32),
            pltpu.VMEM(reply.shape, BF16),
            pltpu.VMEM(partial.shape, BF16),
            pltpu.SMEM((WIN,), jnp.int32),
            pltpu.SemaphoreType.DMA((2,)),
            pltpu.SemaphoreType.DMA((blocks // 2,)),
            pltpu.SemaphoreType.DMA((blocks // 2,)),
        ],
        compiler_params=room_for(reply),
        cost_estimate=pl.CostEstimate(flops=1 << 25, bytes_accessed=4 << 20, transcendentals=0),
    )(pool_owner, partial, reply)


def per_device(
    fine_nodes,
    edge_tiles,
    edge_target,
    edge_source,
    edge_count,
    halo_blocks,
    pool_owner,
    coarse_tiles,
    pooled_block_source_index,
    fine_first,
    fine_bias,
    fine_second,
    fine_gain,
    coarse_first,
    coarse_bias,
    coarse_second,
    pooled_level_scale_factor,
):
    block_count = pool_owner.shape[0]
    rows = edge_tiles.shape[1]
    width = fine_nodes.shape[1]
    subs = lax.axis_size("sub")
    everyone = ("win", "mem", "sub")
    devices = lax.axis_size(everyone)
    blocks = fine_nodes.reshape(block_count, rows, width)

    own_sub = lax.axis_index("sub").astype(jnp.int32)[None]
    index = lax.axis_index(everyone)
    late = ((index % ROW == ROW - 1) & (index < devices - 1)).astype(jnp.int32)[None]
    send, lower, upper = pack(pool_owner, halo_blocks, blocks, subs)
    from_lower = lax.ppermute(upper, everyone, [(i, i + 1) for i in range(devices - 1)])
    from_upper = lax.ppermute(
        lower, everyone, [(i + 1, i) for i in range(devices - 1) if (i + 1) % ROW]
    )
    arrived = lax.all_to_all(send, ("mem", "sub"), 0, 0, tiled=True)
    entries = (edge_target, edge_source, edge_count)
    network_in = (edge_tiles, blocks, fine_first, fine_bias, fine_second, fine_gain)
    done = fine_update(late, entries, from_lower, from_upper, *network_in)
    lower, done = lax.optimization_barrier((lower, done))
    late_upper = lax.ppermute(lower, everyone, [(i, i - 1) for i in range(ROW, devices, ROW)])
    reply = coarse_update(
        own_sub,
        pooled_block_source_index,
        arrived,
        coarse_tiles,
        coarse_first,
        coarse_bias,
        coarse_second,
        pooled_level_scale_factor,
        done,
    )
    returned = lax.all_to_all(reply, "mem", 0, 0, tiled=True)
    partial = fine_update(late, entries, from_lower, late_upper, *network_in, done=done, after=reply)
    return finish(pool_owner, partial, returned).reshape(fine_nodes.shape)


def solution(mesh):
    dom, sub = mesh.devices.shape
    split = Mesh(mesh.devices.reshape(dom // WIN, WIN, sub), ("win", "mem", "sub"))
    every = ("win", "mem", "sub")
    placed = (
        P(every, None),
        P(every, None, None),
        P(every),
        P(every),
        P(every),
        P(every),
        P(every),
        P(every, None, None),
        P(every),
        P(),
        P(),
        P(),
        P(),
        P(),
        P(),
        P(),
        P(),
    )
    return jax.shard_map(
        per_device, mesh=split, in_specs=placed, out_specs=P(every, None), check_vma=False
    )
```

```python
import jax
import jax.numpy as jnp
from jax import lax
from jax.experimental import pallas as pl
from jax.experimental.pallas import tpu as pltpu
from jax.sharding import Mesh
from jax.sharding import PartitionSpec as P

POOL = 8
WIN = 4
ROW = 64
DEPTH = 2
SIDE = 2
F32 = jnp.float32
BF16 = jnp.bfloat16

VMEM_SPEC = pl.BlockSpec(memory_space=pltpu.VMEM)
SMEM_SPEC = pl.BlockSpec(memory_space=pltpu.SMEM)
HBM_SPEC = pl.BlockSpec(memory_space=pltpu.HBM)
ANY_SPEC = pl.BlockSpec(memory_space=pl.ANY)


PARAMS = pltpu.CompilerParams(vmem_limit_bytes=32 << 20)


def held_in_hbm(*arrays):
    return [pltpu.with_memory_space_constraint(array, pltpu.HBM) for array in arrays]


def started(pairs, sems):
    copies = [pltpu.make_async_copy(src, dst, sems.at[i]) for i, (src, dst) in enumerate(pairs)]
    for copy in copies:
        copy.start()
    return copies


def owner_slots(owner_ref, count_ref, block_count):
    for d in range(WIN):
        count_ref[d] = 0
    slots = []
    for k in range(block_count):
        d = owner_ref[k] & (WIN - 1)
        r = count_ref[d]
        count_ref[d] = r + 1
        slots.append((d, r))
    return slots


def pack_kernel(
    owner_hbm, halo_hbm, nodes_hbm, send_ref, lower_ref, upper_ref,
    owner_ref, halo_ref, nodes_ref, count_ref, index_ref, int_sems, node_sems,
):
    blocks, rows, width = nodes_ref.shape
    tile = rows // POOL
    lanes = send_ref.shape[-1]
    groups = width // lanes
    subs = send_ref.shape[0] // WIN
    halo = lower_ref.shape[0]
    ints = started([(owner_hbm, owner_ref), (halo_hbm, halo_ref)], int_sems)
    loads = started([(nodes_hbm.at[k], nodes_ref.at[k]) for k in range(blocks)], node_sems)
    row = lax.broadcasted_iota(jnp.int32, (tile, rows), 0)
    col = lax.broadcasted_iota(jnp.int32, (tile, rows), 1)
    average = jnp.where(col // POOL == row, 1.0 / POOL, 0.0).astype(BF16)
    for copy in ints:
        copy.wait()
    slots = owner_slots(owner_ref, count_ref, blocks)
    for k, (d, r) in enumerate(slots):
        index_ref[d * 2 + r] = k
    lane = lax.broadcasted_iota(jnp.int32, (tile, lanes), 1)
    for d in range(WIN):
        tag = jnp.where((lane // tile) % 2 == 0, index_ref[2 * d], index_ref[2 * d + 1])
        tag = tag.astype(F32).astype(BF16)
        for s in range(subs):
            send_ref[d * subs + s, groups * 2] = tag
    for k, (d, r) in enumerate(slots):
        loads[k].wait()
        pooled = jnp.dot(average, nodes_ref[k], preferred_element_type=F32).astype(BF16)
        for s in range(subs):
            for c in range(groups):
                send_ref[d * subs + s, c * 2 + r] = pooled[:, c * lanes : (c + 1) * lanes]
    for h in range(halo):
        lower_ref[h] = nodes_ref[halo_ref[h]]
        upper_ref[h] = nodes_ref[halo_ref[halo + h]]


def pack(pool_owner, halo_blocks, blocks, subs):
    count, rows, width = blocks.shape
    tile = rows // POOL
    halos = halo_blocks.shape[0]
    lanes = 128
    pieces = 2 * (width // lanes) + 1
    return pl.pallas_call(
        pack_kernel,
        name="pack",
        out_shape=(
            jax.ShapeDtypeStruct((WIN * subs, pieces, tile, lanes), BF16),
            jax.ShapeDtypeStruct((halos // 2, rows, width), BF16),
            jax.ShapeDtypeStruct((halos // 2, rows, width), BF16),
        ),
        in_specs=[HBM_SPEC] * 3,
        out_specs=(VMEM_SPEC,) * 3,
        scratch_shapes=[
            pltpu.SMEM((count,), jnp.int32),
            pltpu.SMEM((halos,), jnp.int32),
            pltpu.VMEM(blocks.shape, BF16),
            pltpu.SMEM((WIN,), jnp.int32),
            pltpu.SMEM((2 * WIN,), jnp.int32),
            pltpu.SemaphoreType.DMA((2,)),
            pltpu.SemaphoreType.DMA((count,)),
        ],
        compiler_params=PARAMS,
        cost_estimate=pl.CostEstimate(flops=1 << 27, bytes_accessed=3 << 20, transcendentals=0),
    )(*held_in_hbm(pool_owner, halo_blocks, blocks))


def normalised(values, gain):
    row_mean = jnp.mean(values, axis=-1, keepdims=True)
    centred = values - row_mean
    variance = jnp.mean(centred * centred, axis=-1, keepdims=True)
    return centred * lax.rsqrt(variance + 1e-05) * gain


def network(nodes, messages, first_ref, bias_ref, second_ref, gain_ref):
    width = nodes.shape[1]
    hidden = jnp.dot(nodes, first_ref[:width], preferred_element_type=F32)
    hidden += jnp.dot(messages, first_ref[width:], preferred_element_type=F32)
    hidden = jnp.maximum(hidden + bias_ref[...], 0.0).astype(BF16)
    projected = jnp.dot(hidden, second_ref[...], preferred_element_type=F32)
    return normalised(projected, gain_ref[...])


def coarse_kernel(
    sub_ref, offset_hbm, second_hbm, arrived_ref, tiles_ref, first_ref, bias_ref, gain_ref, reply_ref,
    offset_ref, second_ref, sems,
):
    senders, pieces, tile, lanes = arrived_ref.shape
    groups = pieces // 2
    subs = senders // WIN
    entries, rows, _ = tiles_ref.shape
    loads = started([(offset_hbm, offset_ref), (second_hbm, second_ref)], sems)
    row = lax.broadcasted_iota(jnp.int32, (rows, rows), 0)
    col = lax.broadcasted_iota(jnp.int32, (rows, rows), 1)
    same_row = row % tile == col % tile

    def arrived_rows(s):
        return jnp.concatenate(
            [
                jnp.concatenate([arrived_ref[m * subs + s, c * 2 + r] for c in range(groups)], axis=1)
                for m in range(WIN)
                for r in range(2)
            ],
            axis=0,
        )

    def placing(s):
        tags = jnp.zeros((8, lanes), F32)
        lane = lax.broadcasted_iota(jnp.int32, (8, lanes), 1)
        for m in range(WIN):
            tag = arrived_ref[m * subs + s, groups * 2].astype(F32)[:8]
            tags = jnp.where(lane // (2 * tile) == m, tag, tags)
        return jnp.where(same_row & (row // tile == tags[:1].astype(jnp.int32)), 1.0, 0.0)

    own = sub_ref[0]
    own_rows = arrived_rows(own)
    own_back = placing(own).T.astype(BF16)
    loads[0].wait()
    weights, sources = [], []
    for e in range(entries):
        s = lax.rem(own + offset_ref[e], subs)
        sources.append(arrived_rows(s))
        by_col = jnp.dot(tiles_ref[e], placing(s).astype(BF16), preferred_element_type=F32)
        weights.append(by_col.astype(BF16))
    by_col = jnp.concatenate(weights, axis=1)
    by_both = jnp.dot(own_back, by_col, preferred_element_type=F32).astype(BF16)
    messages = jnp.dot(by_both, jnp.concatenate(sources, axis=0), preferred_element_type=F32)
    loads[1].wait()
    delta = network(own_rows, messages.astype(BF16), first_ref, bias_ref, second_ref, gain_ref)
    delta = delta.astype(BF16)
    for m in range(WIN):
        for r in range(2):
            at = (m * 2 + r) * tile
            reply_ref[m, r] = delta[at : at + tile]


def coarse_update(own_sub, offsets, second, arrived, held):
    return pl.pallas_call(
        coarse_kernel,
        name="coarse",
        out_shape=jax.ShapeDtypeStruct((WIN, 2, arrived.shape[2], second.shape[0]), BF16),
        in_specs=[SMEM_SPEC, HBM_SPEC, HBM_SPEC] + [VMEM_SPEC] * 5,
        out_specs=VMEM_SPEC,
        scratch_shapes=[
            pltpu.SMEM(offsets.shape, jnp.int32),
            pltpu.VMEM(second.shape, BF16),
            pltpu.SemaphoreType.DMA((2,)),
        ],
        compiler_params=PARAMS,
        cost_estimate=pl.CostEstimate(flops=1 << 29, bytes_accessed=3 << 20, transcendentals=0),
    )(own_sub, *held_in_hbm(offsets, second), arrived, *held)


def add_messages(
    target_ref, source_ref, live, table, tiles, total, order, place, loads
):
    blocks = total.shape[0]
    entries = target_ref.shape[0]
    slots = order.shape[0]
    for b in range(blocks + 1):
        place[b] = 0
    for i in range(slots):
        order[i] = entries
    bins = []
    for e in range(entries):
        b = jnp.where(e < live, target_ref[e], blocks)
        place[b] = place[b] + 1
        bins.append(b)
    at = 0
    for b in range(blocks):
        steps = (place[b] + (DEPTH - 1)) // DEPTH
        place[b] = at * DEPTH
        at = at + steps
    place[blocks] = slots - entries
    used = at
    for e in range(entries):
        at = place[bins[e]]
        place[bins[e]] = at + 1
        order[at] = e + (source_ref[e] << 8) + (bins[e] << 16)
    for copy in loads:
        copy.wait()

    @pl.loop(0, (used + (SIDE - 1)) // SIDE)
    def _(i):
        products = []
        for u in range(SIDE):
            codes = [order[(i * SIDE + u) * DEPTH + g] for g in range(DEPTH)]
            left = jnp.concatenate([tiles[code & 255] for code in codes], axis=1)
            right = jnp.concatenate([table[(code >> 8) & 255] for code in codes], axis=0)
            product = jnp.dot(left, right, preferred_element_type=F32)
            products.append((codes[0] >> 16, product))
        for b, product in products:
            total[b] += product


def order_slots(entries, blocks):
    groups = entries // DEPTH + blocks
    return (groups + SIDE - 1) // SIDE * SIDE * DEPTH + entries


def fine_body(
    target_hbm, source_hbm, count_ref, lower_hbm, upper_hbm, edges_hbm, nodes_hbm,
    first_hbm, bias_hbm, second_hbm, gain_hbm,
    target_ref, source_ref, table, tiles, total, order, place,
    first_ref, bias_ref, second_ref, gain_ref, sems, use,
):
    entries = edges_hbm.shape[0]
    halo = lower_hbm.shape[0]
    blocks, rows, width = total.shape
    loads = started(
        [
            (target_hbm, target_ref),
            (source_hbm, source_ref),
            (edges_hbm, tiles.at[pl.ds(0, entries)]),
            (nodes_hbm, table.at[pl.ds(0, blocks)]),
            (lower_hbm, table.at[pl.ds(blocks, halo)]),
            (upper_hbm, table.at[pl.ds(blocks + halo, halo)]),
            (first_hbm, first_ref),
            (second_hbm, second_ref),
            (bias_hbm, bias_ref.at[0]),
            (gain_hbm, gain_ref.at[0]),
        ],
        sems,
    )
    tiles[entries] = jnp.zeros(tiles.shape[1:], BF16)
    total[...] = jnp.zeros_like(total)
    for copy in loads[:2]:
        copy.wait()
    add_messages(target_ref, source_ref, count_ref[0], table, tiles, total, order, place, loads[2:6])
    for copy in loads[6:]:
        copy.wait()
    for i in range(blocks // 2):
        nodes = table[2 * i : 2 * i + 2].reshape(2 * rows, width)
        messages = total[2 * i : 2 * i + 2].reshape(2 * rows, width).astype(BF16)
        use(i, nodes.astype(F32) + network(nodes, messages, first_ref, bias_ref, second_ref, gain_ref))


def fine_scratch(edges, nodes, halo, first, second):
    entries, rows, _ = edges.shape
    blocks, _, width = nodes.shape
    return [
        pltpu.SMEM((entries,), jnp.int32),
        pltpu.SMEM((entries,), jnp.int32),
        pltpu.VMEM((blocks + 2 * halo, rows, width), BF16),
        pltpu.VMEM((entries + 1, rows, rows), BF16),
        pltpu.VMEM(nodes.shape, F32),
        pltpu.SMEM((order_slots(entries, blocks),), jnp.int32),
        pltpu.SMEM((blocks + 1,), jnp.int32),
        pltpu.VMEM(first.shape, BF16),
        pltpu.VMEM((1, width), F32),
        pltpu.VMEM(second.shape, BF16),
        pltpu.VMEM((1, width), F32),
        pltpu.SemaphoreType.DMA((10,)),
    ]


FINE_SPECS = [HBM_SPEC, HBM_SPEC, SMEM_SPEC, ANY_SPEC, ANY_SPEC] + [HBM_SPEC] * 6


def fine_inputs(entries, lower, upper, edges, nodes, first, bias, second, gain):
    target, source, count = entries
    return [
        *held_in_hbm(target, source),
        count,
        lower,
        upper,
        *held_in_hbm(edges, nodes, first, bias, second, gain),
    ]


def fine_kernel(late_ref, owner_hbm, *refs):
    coarse_hbm, fine_in, outs, scratch = refs[:4], refs[4:15], refs[15:21], refs[21:]
    partial_ref, slot_ref, *coarse_refs = outs
    *fine_refs, owner_ref, count_ref, sems = scratch
    blocks, rows, width = partial_ref.shape
    tile = rows // POOL
    loads = started(
        [(owner_hbm, owner_ref)]
        + [
            (src, dst.at[0] if dst.shape != src.shape else dst)
            for src, dst in zip(coarse_hbm, coarse_refs)
        ],
        sems,
    )
    loads[0].wait()
    for k, (d, r) in enumerate(owner_slots(owner_ref, count_ref, blocks)):
        slot_ref[k] = jnp.full(slot_ref.shape[1:], (d * 2 + r) * tile, jnp.int32)

    @pl.when(late_ref[0] == 0)
    def _():
        def use(i, values):
            partial_ref[2 * i : 2 * i + 2] = values.astype(BF16).reshape(2, rows, width)

        fine_body(*fine_in, *fine_refs, use)

    for copy in loads[1:]:
        copy.wait()


def fine_update(late, pool_owner, coarse, fine_in):
    edges, nodes, first, _, second, _ = fine_in[5:]
    blocks, rows, width = nodes.shape
    tiles, coarse_first, _, _ = coarse
    partial, slots, *held = pl.pallas_call(
        fine_kernel,
        name="fine",
        out_shape=(
            jax.ShapeDtypeStruct(nodes.shape, BF16),
            jax.ShapeDtypeStruct((blocks, 8, rows), jnp.int32),
            jax.ShapeDtypeStruct(tiles.shape, BF16),
            jax.ShapeDtypeStruct(coarse_first.shape, BF16),
            jax.ShapeDtypeStruct((1, width), F32),
            jax.ShapeDtypeStruct((1, width), F32),
        ),
        in_specs=[SMEM_SPEC] + [HBM_SPEC] * 5 + FINE_SPECS,
        out_specs=(VMEM_SPEC,) * 6,
        scratch_shapes=fine_scratch(edges, nodes, fine_in[3].shape[0], first, second)
        + [pltpu.SMEM((blocks,), jnp.int32), pltpu.SMEM((WIN,), jnp.int32), pltpu.SemaphoreType.DMA((5,))],
        compiler_params=PARAMS,
        cost_estimate=pl.CostEstimate(flops=1 << 37, bytes_accessed=1 << 20, transcendentals=0),
    )(late, *held_in_hbm(pool_owner, *coarse), *fine_in)
    return partial, slots, held


def finish_kernel(late_ref, partial_ref, slot_ref, reply_ref, *refs):
    fine_in, out_hbm, (*fine_refs, out_ref, out_sems) = refs[:11], refs[11], refs[12:]
    blocks, rows, width = partial_ref.shape
    row = lax.broadcasted_iota(jnp.int32, (rows, rows), 0)
    col = lax.broadcasted_iota(jnp.int32, (rows, rows), 1)
    place = col - row // POOL

    def use(i, values):
        at = pl.ds(2 * i, 2)
        spread = [jnp.where(place == slot_ref[k][:1], 1.0, 0.0) for k in (2 * i, 2 * i + 1)]
        spread = jnp.concatenate(spread, axis=0).astype(BF16)
        back = jnp.dot(spread, reply_ref[...].reshape(rows, width), preferred_element_type=F32)
        out_ref[2 * i : 2 * i + 2] = (values + back).astype(BF16).reshape(2, rows, width)
        started([(out_ref.at[at], out_hbm.at[at])], out_sems.at[pl.ds(i, 1)])

    @pl.when(late_ref[0] == 0)
    def _():
        for i in range(blocks // 2):
            use(i, partial_ref[2 * i : 2 * i + 2].reshape(2 * rows, width).astype(F32))

    @pl.when(late_ref[0] == 1)
    def _():
        fine_body(*fine_in, *fine_refs, use)

    for i in range(blocks // 2):
        at = pl.ds(2 * i, 2)
        pltpu.make_async_copy(out_ref.at[at], out_hbm.at[at], out_sems.at[i]).wait()


def finish(late, partial, slots, reply, fine_in):
    edges, nodes, first, _, second, _ = fine_in[5:]
    return pl.pallas_call(
        finish_kernel,
        name="finish",
        out_shape=jax.ShapeDtypeStruct(partial.shape, BF16),
        in_specs=[SMEM_SPEC] + [VMEM_SPEC] * 3 + FINE_SPECS,
        out_specs=ANY_SPEC,
        scratch_shapes=fine_scratch(edges, nodes, fine_in[3].shape[0], first, second)
        + [pltpu.VMEM(partial.shape, BF16), pltpu.SemaphoreType.DMA((partial.shape[0] // 2,))],
        compiler_params=PARAMS,
        cost_estimate=pl.CostEstimate(flops=1 << 25, bytes_accessed=4 << 20, transcendentals=0),
    )(late, partial, slots, reply, *fine_in)


def per_device(
    fine_nodes,
    edge_tiles,
    edge_target,
    edge_source,
    edge_count,
    halo_blocks,
    pool_owner,
    coarse_tiles,
    pooled_block_source_index,
    fine_first,
    fine_bias,
    fine_second,
    fine_gain,
    coarse_first,
    coarse_bias,
    coarse_second,
    pooled_level_scale_factor,
):
    block_count = pool_owner.shape[0]
    rows = edge_tiles.shape[1]
    width = fine_nodes.shape[1]
    subs = lax.axis_size("sub")
    everyone = ("win", "mem", "sub")
    devices = lax.axis_size(everyone)
    blocks = fine_nodes.reshape(block_count, rows, width)

    own_sub = lax.axis_index("sub").astype(jnp.int32)[None]
    index = lax.axis_index(everyone)
    late = ((index % ROW == ROW - 1) & (index < devices - 1)).astype(jnp.int32)[None]
    send, lower, upper = pack(pool_owner, halo_blocks, blocks, subs)
    from_lower = lax.ppermute(upper, everyone, [(i, i + 1) for i in range(devices - 1)])
    from_upper = lax.ppermute(
        lower, everyone, [(i + 1, i) for i in range(devices - 1) if (i + 1) % ROW]
    )
    arrived = lax.all_to_all(send, ("mem", "sub"), 0, 0, tiled=True)
    entries = (edge_target, edge_source, edge_count)
    network_in = (edge_tiles, blocks, fine_first, fine_bias, fine_second, fine_gain)
    coarse_in = (coarse_tiles, coarse_first, coarse_bias, pooled_level_scale_factor)
    partial, slots, held = fine_update(
        late, pool_owner, coarse_in, fine_inputs(entries, from_lower, from_upper, *network_in)
    )
    lower, partial = lax.optimization_barrier((lower, partial))
    late_upper = lax.ppermute(lower, everyone, [(i, i - 1) for i in range(ROW, devices, ROW)])
    reply = coarse_update(own_sub, pooled_block_source_index, coarse_second, arrived, held)
    returned = lax.all_to_all(reply, "mem", 0, 0, tiled=True)
    late_in = fine_inputs(entries, from_lower, late_upper, *network_in)
    return finish(late, partial, slots, returned, late_in).reshape(fine_nodes.shape)


def solution(mesh):
    dom, sub = mesh.devices.shape
    split = Mesh(mesh.devices.reshape(dom // WIN, WIN, sub), ("win", "mem", "sub"))
    every = ("win", "mem", "sub")
    placed = (
        P(every, None),
        P(every, None, None),
        P(every),
        P(every),
        P(every),
        P(every),
        P(every),
        P(every, None, None),
        P(every),
        P(),
        P(),
        P(),
        P(),
        P(),
        P(),
        P(),
        P(),
    )
    return jax.shard_map(
        per_device, mesh=split, in_specs=placed, out_specs=P(every, None), check_vma=False
    )
```

```python
import jax
import jax.numpy as jnp
from jax import lax
from jax.experimental import pallas as pl
from jax.experimental.pallas import tpu as pltpu
from jax.sharding import Mesh
from jax.sharding import PartitionSpec as P

POOL = 8
WIN = 4
ROW = 64
DEPTH = 2
SIDE = 4
F32 = jnp.float32
BF16 = jnp.bfloat16

VMEM_SPEC = pl.BlockSpec(memory_space=pltpu.VMEM)
SMEM_SPEC = pl.BlockSpec(memory_space=pltpu.SMEM)
HBM_SPEC = pl.BlockSpec(memory_space=pltpu.HBM)
ANY_SPEC = pl.BlockSpec(memory_space=pl.ANY)


PARAMS = pltpu.CompilerParams(vmem_limit_bytes=32 << 20)


def held_in_hbm(*arrays):
    return [pltpu.with_memory_space_constraint(array, pltpu.HBM) for array in arrays]


def started(pairs, sems):
    copies = [pltpu.make_async_copy(src, dst, sems.at[i]) for i, (src, dst) in enumerate(pairs)]
    for copy in copies:
        copy.start()
    return copies


def owner_slots(owner_ref, count_ref, block_count):
    for d in range(WIN):
        count_ref[d] = 0
    slots = []
    for k in range(block_count):
        d = owner_ref[k] & (WIN - 1)
        r = count_ref[d]
        count_ref[d] = r + 1
        slots.append((d, r))
    return slots


def pack_kernel(
    owner_hbm, halo_hbm, nodes_hbm, first_hbm, tiles_hbm, bias_hbm, gain_hbm,
    send_ref, lower_ref, upper_ref, slot_ref, first_ref, tiles_ref, bias_ref, gain_ref,
    owner_ref, halo_ref, nodes_ref, count_ref, index_ref, int_sems, node_sems, held_sems,
):
    blocks, rows, width = nodes_ref.shape
    tile = rows // POOL
    lanes = send_ref.shape[-1]
    groups = width // lanes
    subs = send_ref.shape[0] // WIN
    halo = lower_ref.shape[0]
    ints = started([(owner_hbm, owner_ref), (halo_hbm, halo_ref)], int_sems)
    loads = started([(nodes_hbm.at[k], nodes_ref.at[k]) for k in range(blocks)], node_sems)
    held = started(
        [
            (first_hbm, first_ref),
            (tiles_hbm, tiles_ref),
            (bias_hbm, bias_ref.at[0]),
            (gain_hbm, gain_ref.at[0]),
        ],
        held_sems,
    )
    row = lax.broadcasted_iota(jnp.int32, (tile, rows), 0)
    col = lax.broadcasted_iota(jnp.int32, (tile, rows), 1)
    average = jnp.where(col // POOL == row, 1.0 / POOL, 0.0).astype(BF16)
    for copy in ints:
        copy.wait()
    slots = owner_slots(owner_ref, count_ref, blocks)
    for k, (d, r) in enumerate(slots):
        index_ref[d * 2 + r] = k
        slot_ref[k] = jnp.full(slot_ref.shape[1:], (d * 2 + r) * tile, jnp.int32)
    lane = lax.broadcasted_iota(jnp.int32, (tile, lanes), 1)
    for d in range(WIN):
        tag = jnp.where((lane // tile) % 2 == 0, index_ref[2 * d], index_ref[2 * d + 1])
        tag = tag.astype(F32).astype(BF16)
        for s in range(subs):
            send_ref[d * subs + s, groups * 2] = tag
    for k, (d, r) in enumerate(slots):
        loads[k].wait()
        pooled = jnp.dot(average, nodes_ref[k], preferred_element_type=F32).astype(BF16)
        for s in range(subs):
            for c in range(groups):
                send_ref[d * subs + s, c * 2 + r] = pooled[:, c * lanes : (c + 1) * lanes]
    for h in range(halo):
        lower_ref[h] = nodes_ref[halo_ref[h]]
        upper_ref[h] = nodes_ref[halo_ref[halo + h]]
    for copy in held:
        copy.wait()


def pack(pool_owner, halo_blocks, blocks, first, tiles, bias, gain, subs):
    count, rows, width = blocks.shape
    tile = rows // POOL
    halos = halo_blocks.shape[0]
    lanes = 128
    pieces = 2 * (width // lanes) + 1
    return pl.pallas_call(
        pack_kernel,
        name="pack",
        out_shape=(
            jax.ShapeDtypeStruct((WIN * subs, pieces, tile, lanes), BF16),
            jax.ShapeDtypeStruct((halos // 2, rows, width), BF16),
            jax.ShapeDtypeStruct((halos // 2, rows, width), BF16),
            jax.ShapeDtypeStruct((count, 8, rows), jnp.int32),
            jax.ShapeDtypeStruct(first.shape, BF16),
            jax.ShapeDtypeStruct(tiles.shape, BF16),
            jax.ShapeDtypeStruct((1, width), F32),
            jax.ShapeDtypeStruct((1, width), F32),
        ),
        in_specs=[HBM_SPEC] * 7,
        out_specs=(VMEM_SPEC,) * 8,
        scratch_shapes=[
            pltpu.SMEM((count,), jnp.int32),
            pltpu.SMEM((halos,), jnp.int32),
            pltpu.VMEM(blocks.shape, BF16),
            pltpu.SMEM((WIN,), jnp.int32),
            pltpu.SMEM((2 * WIN,), jnp.int32),
            pltpu.SemaphoreType.DMA((2,)),
            pltpu.SemaphoreType.DMA((count,)),
            pltpu.SemaphoreType.DMA((4,)),
        ],
        compiler_params=PARAMS,
        cost_estimate=pl.CostEstimate(flops=1 << 27, bytes_accessed=3 << 20, transcendentals=0),
    )(*held_in_hbm(pool_owner, halo_blocks, blocks, first, tiles, bias, gain))


def normalised(values, gain):
    row_mean = jnp.mean(values, axis=-1, keepdims=True)
    centred = values - row_mean
    variance = jnp.mean(centred * centred, axis=-1, keepdims=True)
    return centred * lax.rsqrt(variance + 1e-05) * gain


def network(nodes, messages, first_ref, bias_ref, second_ref, gain_ref):
    width = nodes.shape[1]
    hidden = jnp.dot(nodes, first_ref[:width], preferred_element_type=F32)
    hidden += jnp.dot(messages, first_ref[width:], preferred_element_type=F32)
    hidden = jnp.maximum(hidden + bias_ref[...], 0.0).astype(BF16)
    projected = jnp.dot(hidden, second_ref[...], preferred_element_type=F32)
    return normalised(projected, gain_ref[...])


def coarse_kernel(
    sub_ref, offset_hbm, second_hbm, arrived_ref, first_ref, tiles_ref, bias_ref, gain_ref, reply_ref,
    offset_ref, second_ref, sems,
):
    senders, pieces, tile, lanes = arrived_ref.shape
    groups = pieces // 2
    subs = senders // WIN
    entries, rows, _ = tiles_ref.shape
    loads = started([(offset_hbm, offset_ref), (second_hbm, second_ref)], sems)
    row = lax.broadcasted_iota(jnp.int32, (rows, rows), 0)
    col = lax.broadcasted_iota(jnp.int32, (rows, rows), 1)
    same_row = row % tile == col % tile

    def arrived_rows(s):
        return jnp.concatenate(
            [
                jnp.concatenate([arrived_ref[m * subs + s, c * 2 + r] for c in range(groups)], axis=1)
                for m in range(WIN)
                for r in range(2)
            ],
            axis=0,
        )

    def placing(s):
        tags = jnp.zeros((8, lanes), F32)
        lane = lax.broadcasted_iota(jnp.int32, (8, lanes), 1)
        for m in range(WIN):
            tag = arrived_ref[m * subs + s, groups * 2].astype(F32)[:8]
            tags = jnp.where(lane // (2 * tile) == m, tag, tags)
        return jnp.where(same_row & (row // tile == tags[:1].astype(jnp.int32)), 1.0, 0.0)

    own = sub_ref[0]
    own_rows = arrived_rows(own)
    own_back = placing(own).T.astype(BF16)
    loads[0].wait()
    weights, sources = [], []
    for e in range(entries):
        s = lax.rem(own + offset_ref[e], subs)
        sources.append(arrived_rows(s))
        by_col = jnp.dot(tiles_ref[e], placing(s).astype(BF16), preferred_element_type=F32)
        weights.append(by_col.astype(BF16))
    by_col = jnp.concatenate(weights, axis=1)
    by_both = jnp.dot(own_back, by_col, preferred_element_type=F32).astype(BF16)
    messages = jnp.dot(by_both, jnp.concatenate(sources, axis=0), preferred_element_type=F32)
    loads[1].wait()
    delta = network(own_rows, messages.astype(BF16), first_ref, bias_ref, second_ref, gain_ref)
    delta = delta.astype(BF16)
    for m in range(WIN):
        for r in range(2):
            at = (m * 2 + r) * tile
            reply_ref[m, r] = delta[at : at + tile]


def coarse_update(own_sub, offsets, second, arrived, held):
    return pl.pallas_call(
        coarse_kernel,
        name="coarse",
        out_shape=jax.ShapeDtypeStruct((WIN, 2, arrived.shape[2], second.shape[0]), BF16),
        in_specs=[SMEM_SPEC, HBM_SPEC, HBM_SPEC] + [VMEM_SPEC] * 5,
        out_specs=VMEM_SPEC,
        scratch_shapes=[
            pltpu.SMEM(offsets.shape, jnp.int32),
            pltpu.VMEM(second.shape, BF16),
            pltpu.SemaphoreType.DMA((2,)),
        ],
        compiler_params=PARAMS,
        cost_estimate=pl.CostEstimate(flops=1 << 29, bytes_accessed=3 << 20, transcendentals=0),
    )(own_sub, *held_in_hbm(offsets, second), arrived, *held)


def add_messages(
    target_ref, source_ref, live, table, tiles, total, order, place, loads
):
    blocks = total.shape[0]
    entries = target_ref.shape[0]
    slots = order.shape[0]
    for b in range(blocks + 1):
        place[b] = 0
    for i in range(slots):
        order[i] = entries
    bins = []
    for e in range(entries):
        b = jnp.where(e < live, target_ref[e], blocks)
        place[b] = place[b] + 1
        bins.append(b)
    at = 0
    for b in range(blocks):
        steps = (place[b] + (DEPTH - 1)) // DEPTH
        place[b] = at * DEPTH
        at = at + steps
    place[blocks] = slots - entries
    used = at
    for e in range(entries):
        at = place[bins[e]]
        place[bins[e]] = at + 1
        order[at] = e + (source_ref[e] << 8) + (bins[e] << 16)
    for copy in loads:
        copy.wait()

    @pl.loop(0, (used + (SIDE - 1)) // SIDE)
    def _(i):
        products = []
        for u in range(SIDE):
            codes = [order[(i * SIDE + u) * DEPTH + g] for g in range(DEPTH)]
            left = jnp.concatenate([tiles[code & 255] for code in codes], axis=1)
            right = jnp.concatenate([table[(code >> 8) & 255] for code in codes], axis=0)
            product = jnp.dot(left, right, preferred_element_type=F32)
            products.append((codes[0] >> 16, product))
        for b, product in products:
            total[b] += product


def order_slots(entries, blocks):
    groups = entries // DEPTH + blocks
    return (groups + SIDE - 1) // SIDE * SIDE * DEPTH + entries


def fine_body(
    target_hbm, source_hbm, count_ref, lower_hbm, upper_hbm, edges_hbm, nodes_hbm,
    first_hbm, bias_hbm, second_hbm, gain_hbm,
    target_ref, source_ref, table, tiles, total, order, place,
    first_ref, bias_ref, second_ref, gain_ref, sems, use,
):
    entries = edges_hbm.shape[0]
    halo = lower_hbm.shape[0]
    blocks, rows, width = total.shape
    loads = started(
        [
            (target_hbm, target_ref),
            (source_hbm, source_ref),
            (edges_hbm, tiles.at[pl.ds(0, entries)]),
            (nodes_hbm, table.at[pl.ds(0, blocks)]),
            (lower_hbm, table.at[pl.ds(blocks, halo)]),
            (upper_hbm, table.at[pl.ds(blocks + halo, halo)]),
            (first_hbm, first_ref),
            (second_hbm, second_ref),
            (bias_hbm, bias_ref.at[0]),
            (gain_hbm, gain_ref.at[0]),
        ],
        sems,
    )
    tiles[entries] = jnp.zeros(tiles.shape[1:], BF16)
    total[...] = jnp.zeros_like(total)
    for copy in loads[:2]:
        copy.wait()
    add_messages(target_ref, source_ref, count_ref[0], table, tiles, total, order, place, loads[2:6])
    for copy in loads[6:]:
        copy.wait()
    for i in range(blocks // 2):
        nodes = table[2 * i : 2 * i + 2].reshape(2 * rows, width)
        messages = total[2 * i : 2 * i + 2].reshape(2 * rows, width).astype(BF16)
        use(i, nodes.astype(F32) + network(nodes, messages, first_ref, bias_ref, second_ref, gain_ref))


def fine_scratch(edges, nodes, halo, first, second):
    entries, rows, _ = edges.shape
    blocks, _, width = nodes.shape
    return [
        pltpu.SMEM((entries,), jnp.int32),
        pltpu.SMEM((entries,), jnp.int32),
        pltpu.VMEM((blocks + 2 * halo, rows, width), BF16),
        pltpu.VMEM((entries + 1, rows, rows), BF16),
        pltpu.VMEM(nodes.shape, F32),
        pltpu.SMEM((order_slots(entries, blocks),), jnp.int32),
        pltpu.SMEM((blocks + 1,), jnp.int32),
        pltpu.VMEM(first.shape, BF16),
        pltpu.VMEM((1, width), F32),
        pltpu.VMEM(second.shape, BF16),
        pltpu.VMEM((1, width), F32),
        pltpu.SemaphoreType.DMA((10,)),
    ]


FINE_SPECS = [HBM_SPEC, HBM_SPEC, SMEM_SPEC, ANY_SPEC, ANY_SPEC] + [HBM_SPEC] * 6


def fine_inputs(entries, lower, upper, edges, nodes, first, bias, second, gain):
    target, source, count = entries
    return [
        *held_in_hbm(target, source),
        count,
        lower,
        upper,
        *held_in_hbm(edges, nodes, first, bias, second, gain),
    ]


def fine_kernel(late_ref, *refs):
    fine_in, partial_ref, fine_refs = refs[:11], refs[11], refs[12:]
    _, rows, width = partial_ref.shape

    def use(i, values):
        partial_ref[2 * i : 2 * i + 2] = values.astype(BF16).reshape(2, rows, width)

    @pl.when(late_ref[0] == 0)
    def _():
        fine_body(*fine_in, *fine_refs, use)


def fine_update(late, fine_in):
    edges, nodes, first, _, second, _ = fine_in[5:]
    return pl.pallas_call(
        fine_kernel,
        name="fine",
        out_shape=jax.ShapeDtypeStruct(nodes.shape, BF16),
        in_specs=[SMEM_SPEC] + FINE_SPECS,
        out_specs=VMEM_SPEC,
        scratch_shapes=fine_scratch(edges, nodes, fine_in[3].shape[0], first, second),
        compiler_params=PARAMS,
        cost_estimate=pl.CostEstimate(flops=1 << 37, bytes_accessed=1 << 20, transcendentals=0),
    )(late, *fine_in)


def finish_kernel(late_ref, mem_ref, partial_ref, slot_ref, replies_ref, *refs):
    fine_in, out_hbm, (*fine_refs, out_ref, out_sems) = refs[:11], refs[11], refs[12:]
    blocks, rows, width = partial_ref.shape
    row = lax.broadcasted_iota(jnp.int32, (rows, rows), 0)
    col = lax.broadcasted_iota(jnp.int32, (rows, rows), 1)
    place = col - row // POOL
    mine = [replies_ref[q, mem_ref[0]].reshape(rows // WIN, width) for q in range(WIN)]
    reply = jnp.concatenate(mine, axis=0)

    def use(i, values):
        at = pl.ds(2 * i, 2)
        spread = [jnp.where(place == slot_ref[k][:1], 1.0, 0.0) for k in (2 * i, 2 * i + 1)]
        spread = jnp.concatenate(spread, axis=0).astype(BF16)
        back = jnp.dot(spread, reply, preferred_element_type=F32)
        out_ref[2 * i : 2 * i + 2] = (values + back).astype(BF16).reshape(2, rows, width)
        started([(out_ref.at[at], out_hbm.at[at])], out_sems.at[pl.ds(i, 1)])

    @pl.when(late_ref[0] == 0)
    def _():
        for i in range(blocks // 2):
            use(i, partial_ref[2 * i : 2 * i + 2].reshape(2 * rows, width).astype(F32))

    @pl.when(late_ref[0] == 1)
    def _():
        fine_body(*fine_in, *fine_refs, use)

    for i in range(blocks // 2):
        at = pl.ds(2 * i, 2)
        pltpu.make_async_copy(out_ref.at[at], out_hbm.at[at], out_sems.at[i]).wait()


def finish(late, own_mem, partial, slots, replies, fine_in):
    edges, nodes, first, _, second, _ = fine_in[5:]
    return pl.pallas_call(
        finish_kernel,
        name="finish",
        out_shape=jax.ShapeDtypeStruct(partial.shape, BF16),
        in_specs=[SMEM_SPEC] * 2 + [VMEM_SPEC] * 3 + FINE_SPECS,
        out_specs=ANY_SPEC,
        scratch_shapes=fine_scratch(edges, nodes, fine_in[3].shape[0], first, second)
        + [pltpu.VMEM(partial.shape, BF16), pltpu.SemaphoreType.DMA((partial.shape[0] // 2,))],
        compiler_params=PARAMS,
        cost_estimate=pl.CostEstimate(flops=1 << 25, bytes_accessed=4 << 20, transcendentals=0),
    )(late, own_mem, partial, slots, replies, *fine_in)


def per_device(
    fine_nodes,
    edge_tiles,
    edge_target,
    edge_source,
    edge_count,
    halo_blocks,
    pool_owner,
    coarse_tiles,
    pooled_block_source_index,
    fine_first,
    fine_bias,
    fine_second,
    fine_gain,
    coarse_first,
    coarse_bias,
    coarse_second,
    pooled_level_scale_factor,
):
    block_count = pool_owner.shape[0]
    rows = edge_tiles.shape[1]
    width = fine_nodes.shape[1]
    subs = lax.axis_size("sub")
    everyone = ("win", "mem", "sub")
    devices = lax.axis_size(everyone)
    blocks = fine_nodes.reshape(block_count, rows, width)

    own_sub = lax.axis_index("sub").astype(jnp.int32)[None]
    index = lax.axis_index(everyone)
    late = ((index % ROW == ROW - 1) & (index < devices - 1)).astype(jnp.int32)[None]
    send, lower, upper, slots, *held = pack(
        pool_owner,
        halo_blocks,
        blocks,
        coarse_first,
        coarse_tiles,
        coarse_bias,
        pooled_level_scale_factor,
        subs,
    )
    from_lower = lax.ppermute(upper, everyone, [(i, i + 1) for i in range(devices - 1)])
    from_upper = lax.ppermute(
        lower, everyone, [(i + 1, i) for i in range(devices - 1) if (i + 1) % ROW]
    )
    arrived = lax.all_to_all(send, ("mem", "sub"), 0, 0, tiled=True)
    entries = (edge_target, edge_source, edge_count)
    network_in = (edge_tiles, blocks, fine_first, fine_bias, fine_second, fine_gain)
    partial = fine_update(late, fine_inputs(entries, from_lower, from_upper, *network_in))
    lower, partial = lax.optimization_barrier((lower, partial))
    late_upper = lax.ppermute(lower, everyone, [(i, i - 1) for i in range(ROW, devices, ROW)])
    reply = coarse_update(own_sub, pooled_block_source_index, coarse_second, arrived, held)
    replies = lax.all_gather(reply, "mem")
    own_mem = lax.axis_index("mem").astype(jnp.int32)[None]
    late_in = fine_inputs(entries, from_lower, late_upper, *network_in)
    return finish(late, own_mem, partial, slots, replies, late_in).reshape(fine_nodes.shape)


def solution(mesh):
    dom, sub = mesh.devices.shape
    split = Mesh(mesh.devices.reshape(dom // WIN, WIN, sub), ("win", "mem", "sub"))
    every = ("win", "mem", "sub")
    placed = (
        P(every, None),
        P(every, None, None),
        P(every),
        P(every),
        P(every),
        P(every),
        P(every),
        P(every, None, None),
        P(every),
        P(),
        P(),
        P(),
        P(),
        P(),
        P(),
        P(),
        P(),
    )
    return jax.shard_map(
        per_device, mesh=split, in_specs=placed, out_specs=P(every, None), check_vma=False
    )
```

```python
import jax
import jax.numpy as jnp
from jax import lax
from jax.experimental import pallas as pl
from jax.experimental.pallas import tpu as pltpu
from jax.sharding import Mesh
from jax.sharding import PartitionSpec as P

POOL = 8
WIN = 4
ROW = 64
PARTS = 2
DEPTH = 2
SIDE = 4
F32 = jnp.float32
BF16 = jnp.bfloat16

VMEM_SPEC = pl.BlockSpec(memory_space=pltpu.VMEM)
SMEM_SPEC = pl.BlockSpec(memory_space=pltpu.SMEM)
HBM_SPEC = pl.BlockSpec(memory_space=pltpu.HBM)
ANY_SPEC = pl.BlockSpec(memory_space=pl.ANY)


PARAMS = pltpu.CompilerParams(vmem_limit_bytes=32 << 20)


def held_in_hbm(*arrays):
    return [pltpu.with_memory_space_constraint(array, pltpu.HBM) for array in arrays]


def started(pairs, sems):
    copies = [pltpu.make_async_copy(src, dst, sems.at[i]) for i, (src, dst) in enumerate(pairs)]
    for copy in copies:
        copy.start()
    return copies


def owner_slots(owner_ref, count_ref, block_count):
    for d in range(WIN):
        count_ref[d] = 0
    slots = []
    for k in range(block_count):
        d = owner_ref[k] & (WIN - 1)
        r = count_ref[d]
        count_ref[d] = r + 1
        slots.append((d, r))
    return slots


def pack_kernel(
    owner_hbm, halo_hbm, nodes_hbm, first_hbm, tiles_hbm, bias_hbm, gain_hbm,
    send_ref, lower_ref, upper_ref, slot_ref, first_ref, tiles_ref, bias_ref, gain_ref,
    owner_ref, halo_ref, nodes_ref, count_ref, index_ref, int_sems, node_sems, held_sems,
):
    blocks, rows, width = nodes_ref.shape
    tile = rows // POOL
    lanes = send_ref.shape[-1]
    groups = width // lanes
    subs = send_ref.shape[0] // WIN
    halo = lower_ref.shape[0]
    ints = started([(owner_hbm, owner_ref), (halo_hbm, halo_ref)], int_sems)
    parts = [pl.ds(at, blocks // PARTS) for at in range(0, blocks, blocks // PARTS)]
    loads = started([(nodes_hbm.at[part], nodes_ref.at[part]) for part in parts], node_sems)
    held = started(
        [
            (first_hbm, first_ref),
            (tiles_hbm, tiles_ref),
            (bias_hbm, bias_ref.at[0]),
            (gain_hbm, gain_ref.at[0]),
        ],
        held_sems,
    )
    few = blocks // PARTS
    row = lax.broadcasted_iota(jnp.int32, (few * tile, few * rows), 0)
    col = lax.broadcasted_iota(jnp.int32, (few * tile, few * rows), 1)
    average = jnp.where(col // POOL == row, 1.0 / POOL, 0.0).astype(BF16)
    for copy in ints:
        copy.wait()
    slots = owner_slots(owner_ref, count_ref, blocks)
    for k, (d, r) in enumerate(slots):
        index_ref[d * 2 + r] = k
        slot_ref[k] = jnp.full(slot_ref.shape[1:], (d * 2 + r) * tile, jnp.int32)
    lane = lax.broadcasted_iota(jnp.int32, (tile, lanes), 1)
    for d in range(WIN):
        tag = jnp.where((lane // tile) % 2 == 0, index_ref[2 * d], index_ref[2 * d + 1])
        tag = tag.astype(F32).astype(BF16)
        for s in range(subs):
            send_ref[d * subs + s, groups * 2] = tag
    for part, load in enumerate(loads):
        load.wait()
        nodes = nodes_ref[part * few : (part + 1) * few].reshape(few * rows, width)
        pooled = jnp.dot(average, nodes, preferred_element_type=F32).astype(BF16)
        for k, (d, r) in enumerate(slots[part * few : (part + 1) * few]):
            for s in range(subs):
                for c in range(groups):
                    piece = pooled[k * tile : (k + 1) * tile, c * lanes : (c + 1) * lanes]
                    send_ref[d * subs + s, c * 2 + r] = piece
    for h in range(halo):
        lower_ref[h] = nodes_ref[halo_ref[h]]
        upper_ref[h] = nodes_ref[halo_ref[halo + h]]
    for copy in held:
        copy.wait()


def pack(pool_owner, halo_blocks, blocks, first, tiles, bias, gain, subs):
    count, rows, width = blocks.shape
    tile = rows // POOL
    halos = halo_blocks.shape[0]
    lanes = 128
    pieces = 2 * (width // lanes) + 1
    return pl.pallas_call(
        pack_kernel,
        name="pack",
        out_shape=(
            jax.ShapeDtypeStruct((WIN * subs, pieces, tile, lanes), BF16),
            jax.ShapeDtypeStruct((halos // 2, rows, width), BF16),
            jax.ShapeDtypeStruct((halos // 2, rows, width), BF16),
            jax.ShapeDtypeStruct((count, 8, rows), jnp.int32),
            jax.ShapeDtypeStruct(first.shape, BF16),
            jax.ShapeDtypeStruct(tiles.shape, BF16),
            jax.ShapeDtypeStruct((1, width), F32),
            jax.ShapeDtypeStruct((1, width), F32),
        ),
        in_specs=[HBM_SPEC] * 7,
        out_specs=(VMEM_SPEC,) * 8,
        scratch_shapes=[
            pltpu.SMEM((count,), jnp.int32),
            pltpu.SMEM((halos,), jnp.int32),
            pltpu.VMEM(blocks.shape, BF16),
            pltpu.SMEM((WIN,), jnp.int32),
            pltpu.SMEM((2 * WIN,), jnp.int32),
            pltpu.SemaphoreType.DMA((2,)),
            pltpu.SemaphoreType.DMA((PARTS,)),
            pltpu.SemaphoreType.DMA((4,)),
        ],
        compiler_params=PARAMS,
        cost_estimate=pl.CostEstimate(flops=1 << 27, bytes_accessed=3 << 20, transcendentals=0),
    )(*held_in_hbm(pool_owner, halo_blocks, blocks, first, tiles, bias, gain))


def normalised(values, gain):
    row_mean = jnp.mean(values, axis=-1, keepdims=True)
    centred = values - row_mean
    variance = jnp.mean(centred * centred, axis=-1, keepdims=True)
    return centred * lax.rsqrt(variance + 1e-05) * gain


def network(nodes, messages, first_ref, bias_ref, second_ref, gain_ref):
    width = nodes.shape[1]
    hidden = jnp.dot(nodes, first_ref[:width], preferred_element_type=F32)
    hidden += jnp.dot(messages, first_ref[width:], preferred_element_type=F32)
    hidden = jnp.maximum(hidden + bias_ref[...], 0.0).astype(BF16)
    projected = jnp.dot(hidden, second_ref[...], preferred_element_type=F32)
    return normalised(projected, gain_ref[...])


def coarse_kernel(
    sub_ref, offset_hbm, second_hbm, arrived_ref, first_ref, tiles_ref, bias_ref, gain_ref, reply_ref,
    offset_ref, second_ref, sems,
):
    senders, pieces, tile, lanes = arrived_ref.shape
    groups = pieces // 2
    subs = senders // WIN
    entries, rows, _ = tiles_ref.shape
    loads = started([(offset_hbm, offset_ref), (second_hbm, second_ref)], sems)
    row = lax.broadcasted_iota(jnp.int32, (rows, rows), 0)
    col = lax.broadcasted_iota(jnp.int32, (rows, rows), 1)
    same_row = row % tile == col % tile

    def arrived_rows(s):
        return jnp.concatenate(
            [
                jnp.concatenate([arrived_ref[m * subs + s, c * 2 + r] for c in range(groups)], axis=1)
                for m in range(WIN)
                for r in range(2)
            ],
            axis=0,
        )

    def placing(s):
        tags = jnp.zeros((8, lanes), F32)
        lane = lax.broadcasted_iota(jnp.int32, (8, lanes), 1)
        for m in range(WIN):
            tag = arrived_ref[m * subs + s, groups * 2].astype(F32)[:8]
            tags = jnp.where(lane // (2 * tile) == m, tag, tags)
        return jnp.where(same_row & (row // tile == tags[:1].astype(jnp.int32)), 1.0, 0.0)

    own = sub_ref[0]
    own_rows = arrived_rows(own)
    own_back = placing(own).T.astype(BF16)
    loads[0].wait()
    weights, sources = [], []
    for e in range(entries):
        s = lax.rem(own + offset_ref[e], subs)
        sources.append(arrived_rows(s))
        by_col = jnp.dot(tiles_ref[e], placing(s).astype(BF16), preferred_element_type=F32)
        weights.append(by_col.astype(BF16))
    by_col = jnp.concatenate(weights, axis=1)
    by_both = jnp.dot(own_back, by_col, preferred_element_type=F32).astype(BF16)
    messages = jnp.dot(by_both, jnp.concatenate(sources, axis=0), preferred_element_type=F32)
    loads[1].wait()
    delta = network(own_rows, messages.astype(BF16), first_ref, bias_ref, second_ref, gain_ref)
    delta = delta.astype(BF16)
    for m in range(WIN):
        for r in range(2):
            at = (m * 2 + r) * tile
            reply_ref[m, r] = delta[at : at + tile]


def coarse_update(own_sub, offsets, second, arrived, held):
    return pl.pallas_call(
        coarse_kernel,
        name="coarse",
        out_shape=jax.ShapeDtypeStruct((WIN, 2, arrived.shape[2], second.shape[0]), BF16),
        in_specs=[SMEM_SPEC, HBM_SPEC, HBM_SPEC] + [VMEM_SPEC] * 5,
        out_specs=VMEM_SPEC,
        scratch_shapes=[
            pltpu.SMEM(offsets.shape, jnp.int32),
            pltpu.VMEM(second.shape, BF16),
            pltpu.SemaphoreType.DMA((2,)),
        ],
        compiler_params=PARAMS,
        cost_estimate=pl.CostEstimate(flops=1 << 29, bytes_accessed=3 << 20, transcendentals=0),
    )(own_sub, *held_in_hbm(offsets, second), arrived, *held)


def add_messages(
    target_ref, source_ref, live, table, tiles, total, order, place, loads
):
    blocks = total.shape[0]
    entries = target_ref.shape[0]
    slots = order.shape[0]
    for b in range(blocks + 1):
        place[b] = 0
    for i in range(slots):
        order[i] = entries
    bins = []
    for e in range(entries):
        b = jnp.where(e < live, target_ref[e], blocks)
        place[b] = place[b] + 1
        bins.append(b)
    at = 0
    for b in range(blocks):
        steps = (place[b] + (DEPTH - 1)) // DEPTH
        place[b] = at * DEPTH
        at = at + steps
    place[blocks] = slots - entries
    used = at
    for e in range(entries):
        at = place[bins[e]]
        place[bins[e]] = at + 1
        order[at] = e + (source_ref[e] << 8) + (bins[e] << 16)
    for copy in loads:
        copy.wait()

    @pl.loop(0, (used + (SIDE - 1)) // SIDE)
    def _(i):
        products = []
        for u in range(SIDE):
            codes = [order[(i * SIDE + u) * DEPTH + g] for g in range(DEPTH)]
            left = jnp.concatenate([tiles[code & 255] for code in codes], axis=1)
            right = jnp.concatenate([table[(code >> 8) & 255] for code in codes], axis=0)
            product = jnp.dot(left, right, preferred_element_type=F32)
            products.append((codes[0] >> 16, product))
        for b, product in products:
            total[b] += product


def order_slots(entries, blocks):
    groups = entries // DEPTH + blocks
    return (groups + SIDE - 1) // SIDE * SIDE * DEPTH + entries


def fine_body(
    target_hbm, source_hbm, count_ref, lower_hbm, upper_hbm, edges_hbm, nodes_hbm,
    first_hbm, bias_hbm, second_hbm, gain_hbm,
    target_ref, source_ref, table, tiles, total, order, place,
    first_ref, bias_ref, second_ref, gain_ref, sems, use,
):
    entries = edges_hbm.shape[0]
    halo = lower_hbm.shape[0]
    blocks, rows, width = total.shape
    loads = started(
        [
            (target_hbm, target_ref),
            (source_hbm, source_ref),
            (edges_hbm, tiles.at[pl.ds(0, entries)]),
            (nodes_hbm, table.at[pl.ds(0, blocks)]),
            (lower_hbm, table.at[pl.ds(blocks, halo)]),
            (upper_hbm, table.at[pl.ds(blocks + halo, halo)]),
            (first_hbm, first_ref),
            (second_hbm, second_ref),
            (bias_hbm, bias_ref.at[0]),
            (gain_hbm, gain_ref.at[0]),
        ],
        sems,
    )
    tiles[entries] = jnp.zeros(tiles.shape[1:], BF16)
    total[...] = jnp.zeros_like(total)
    for copy in loads[:2]:
        copy.wait()
    add_messages(target_ref, source_ref, count_ref[0], table, tiles, total, order, place, loads[2:6])
    for copy in loads[6:]:
        copy.wait()
    for i in range(blocks // 2):
        nodes = table[2 * i : 2 * i + 2].reshape(2 * rows, width)
        messages = total[2 * i : 2 * i + 2].reshape(2 * rows, width).astype(BF16)
        use(i, nodes.astype(F32) + network(nodes, messages, first_ref, bias_ref, second_ref, gain_ref))


def fine_scratch(edges, nodes, halo, first, second):
    entries, rows, _ = edges.shape
    blocks, _, width = nodes.shape
    return [
        pltpu.SMEM((entries,), jnp.int32),
        pltpu.SMEM((entries,), jnp.int32),
        pltpu.VMEM((blocks + 2 * halo, rows, width), BF16),
        pltpu.VMEM((entries + 1, rows, rows), BF16),
        pltpu.VMEM(nodes.shape, F32),
        pltpu.SMEM((order_slots(entries, blocks),), jnp.int32),
        pltpu.SMEM((blocks + 1,), jnp.int32),
        pltpu.VMEM(first.shape, BF16),
        pltpu.VMEM((1, width), F32),
        pltpu.VMEM(second.shape, BF16),
        pltpu.VMEM((1, width), F32),
        pltpu.SemaphoreType.DMA((10,)),
    ]


FINE_SPECS = [HBM_SPEC, HBM_SPEC, SMEM_SPEC, ANY_SPEC, ANY_SPEC] + [HBM_SPEC] * 6


def fine_inputs(entries, lower, upper, edges, nodes, first, bias, second, gain):
    target, source, count = entries
    return [
        *held_in_hbm(target, source),
        count,
        lower,
        upper,
        *held_in_hbm(edges, nodes, first, bias, second, gain),
    ]


def fine_kernel(late_ref, *refs):
    fine_in, partial_ref, fine_refs = refs[:11], refs[11], refs[12:]
    _, rows, width = partial_ref.shape

    def use(i, values):
        partial_ref[2 * i : 2 * i + 2] = values.astype(BF16).reshape(2, rows, width)

    @pl.when(late_ref[0] == 0)
    def _():
        fine_body(*fine_in, *fine_refs, use)


def fine_update(late, fine_in):
    edges, nodes, first, _, second, _ = fine_in[5:]
    return pl.pallas_call(
        fine_kernel,
        name="fine",
        out_shape=jax.ShapeDtypeStruct(nodes.shape, BF16),
        in_specs=[SMEM_SPEC] + FINE_SPECS,
        out_specs=VMEM_SPEC,
        scratch_shapes=fine_scratch(edges, nodes, fine_in[3].shape[0], first, second),
        compiler_params=PARAMS,
        cost_estimate=pl.CostEstimate(flops=1 << 37, bytes_accessed=1 << 20, transcendentals=0),
    )(late, *fine_in)


def finish_kernel(late_ref, mem_ref, partial_ref, slot_ref, replies_ref, *refs):
    fine_in, out_hbm, (*fine_refs, out_ref, out_sems) = refs[:11], refs[11], refs[12:]
    blocks, rows, width = partial_ref.shape
    row = lax.broadcasted_iota(jnp.int32, (rows, rows), 0)
    col = lax.broadcasted_iota(jnp.int32, (rows, rows), 1)
    place = col - row // POOL
    mine = [replies_ref[q, mem_ref[0]].reshape(rows // WIN, width) for q in range(WIN)]
    reply = jnp.concatenate(mine, axis=0)

    def use(i, values):
        at = pl.ds(2 * i, 2)
        spread = [jnp.where(place == slot_ref[k][:1], 1.0, 0.0) for k in (2 * i, 2 * i + 1)]
        spread = jnp.concatenate(spread, axis=0).astype(BF16)
        back = jnp.dot(spread, reply, preferred_element_type=F32)
        out_ref[2 * i : 2 * i + 2] = (values + back).astype(BF16).reshape(2, rows, width)
        started([(out_ref.at[at], out_hbm.at[at])], out_sems.at[pl.ds(i, 1)])

    @pl.when(late_ref[0] == 0)
    def _():
        for i in range(blocks // 2):
            use(i, partial_ref[2 * i : 2 * i + 2].reshape(2 * rows, width).astype(F32))

    @pl.when(late_ref[0] == 1)
    def _():
        fine_body(*fine_in, *fine_refs, use)

    for i in range(blocks // 2):
        at = pl.ds(2 * i, 2)
        pltpu.make_async_copy(out_ref.at[at], out_hbm.at[at], out_sems.at[i]).wait()


def finish(late, own_mem, partial, slots, replies, fine_in):
    edges, nodes, first, _, second, _ = fine_in[5:]
    return pl.pallas_call(
        finish_kernel,
        name="finish",
        out_shape=jax.ShapeDtypeStruct(partial.shape, BF16),
        in_specs=[SMEM_SPEC] * 2 + [VMEM_SPEC] * 3 + FINE_SPECS,
        out_specs=ANY_SPEC,
        scratch_shapes=fine_scratch(edges, nodes, fine_in[3].shape[0], first, second)
        + [pltpu.VMEM(partial.shape, BF16), pltpu.SemaphoreType.DMA((partial.shape[0] // 2,))],
        compiler_params=PARAMS,
        cost_estimate=pl.CostEstimate(flops=1 << 25, bytes_accessed=4 << 20, transcendentals=0),
    )(late, own_mem, partial, slots, replies, *fine_in)


def per_device(
    fine_nodes,
    edge_tiles,
    edge_target,
    edge_source,
    edge_count,
    halo_blocks,
    pool_owner,
    coarse_tiles,
    pooled_block_source_index,
    fine_first,
    fine_bias,
    fine_second,
    fine_gain,
    coarse_first,
    coarse_bias,
    coarse_second,
    pooled_level_scale_factor,
):
    block_count = pool_owner.shape[0]
    rows = edge_tiles.shape[1]
    width = fine_nodes.shape[1]
    subs = lax.axis_size("sub")
    everyone = ("win", "mem", "sub")
    devices = lax.axis_size(everyone)
    blocks = fine_nodes.reshape(block_count, rows, width)

    own_sub = lax.axis_index("sub").astype(jnp.int32)[None]
    index = lax.axis_index(everyone)
    late = ((index % ROW == ROW - 1) & (index < devices - 1)).astype(jnp.int32)[None]
    send, lower, upper, slots, *held = pack(
        pool_owner,
        halo_blocks,
        blocks,
        coarse_first,
        coarse_tiles,
        coarse_bias,
        pooled_level_scale_factor,
        subs,
    )
    from_lower = lax.ppermute(upper, everyone, [(i, i + 1) for i in range(devices - 1)])
    from_upper = lax.ppermute(
        lower, everyone, [(i + 1, i) for i in range(devices - 1) if (i + 1) % ROW]
    )
    arrived = lax.all_to_all(send, ("mem", "sub"), 0, 0, tiled=True)
    entries = (edge_target, edge_source, edge_count)
    network_in = (edge_tiles, blocks, fine_first, fine_bias, fine_second, fine_gain)
    partial = fine_update(late, fine_inputs(entries, from_lower, from_upper, *network_in))
    lower, partial = lax.optimization_barrier((lower, partial))
    late_upper = lax.ppermute(lower, everyone, [(i, i - 1) for i in range(ROW, devices, ROW)])
    reply = coarse_update(own_sub, pooled_block_source_index, coarse_second, arrived, held)
    replies = lax.all_gather(reply, "mem")
    own_mem = lax.axis_index("mem").astype(jnp.int32)[None]
    late_in = fine_inputs(entries, from_lower, late_upper, *network_in)
    return finish(late, own_mem, partial, slots, replies, late_in).reshape(fine_nodes.shape)


def solution(mesh):
    dom, sub = mesh.devices.shape
    split = Mesh(mesh.devices.reshape(dom // WIN, WIN, sub), ("win", "mem", "sub"))
    every = ("win", "mem", "sub")
    placed = (
        P(every, None),
        P(every, None, None),
        P(every),
        P(every),
        P(every),
        P(every),
        P(every),
        P(every, None, None),
        P(every),
        P(),
        P(),
        P(),
        P(),
        P(),
        P(),
        P(),
        P(),
    )
    return jax.shard_map(
        per_device, mesh=split, in_specs=placed, out_specs=P(every, None), check_vma=False
    )
```

```python
import jax
import jax.numpy as jnp
from jax import lax
from jax.experimental import pallas as pl
from jax.experimental.pallas import tpu as pltpu
from jax.sharding import Mesh
from jax.sharding import PartitionSpec as P

POOL = 8
WIN = 4
ROW = 64
PARTS = 2
DEPTH = 2
SIDE = 4
F32 = jnp.float32
BF16 = jnp.bfloat16

VMEM_SPEC = pl.BlockSpec(memory_space=pltpu.VMEM)
SMEM_SPEC = pl.BlockSpec(memory_space=pltpu.SMEM)
HBM_SPEC = pl.BlockSpec(memory_space=pltpu.HBM)
ANY_SPEC = pl.BlockSpec(memory_space=pl.ANY)


PARAMS = pltpu.CompilerParams(vmem_limit_bytes=32 << 20)


def held_in_hbm(*arrays):
    return [pltpu.with_memory_space_constraint(array, pltpu.HBM) for array in arrays]


def started(pairs, sems):
    copies = [pltpu.make_async_copy(src, dst, sems.at[i]) for i, (src, dst) in enumerate(pairs)]
    for copy in copies:
        copy.start()
    return copies


def owner_slots(owner_ref, count_ref, block_count):
    for d in range(WIN):
        count_ref[d] = 0
    slots = []
    for k in range(block_count):
        d = owner_ref[k] & (WIN - 1)
        r = count_ref[d]
        count_ref[d] = r + 1
        slots.append((d, r))
    return slots


def pack_kernel(
    owner_hbm, halo_hbm, nodes_hbm, first_hbm, tiles_hbm, bias_hbm, gain_hbm,
    send_hbm, lower_hbm, upper_ref, slot_ref, first_ref, tiles_ref, bias_ref, gain_ref,
    owner_ref, halo_ref, nodes_ref, send_ref, count_ref, index_ref,
    int_sems, node_sems, held_sems, lower_sems, send_sems,
):
    blocks, rows, width = nodes_ref.shape
    tile = rows // POOL
    lanes = send_ref.shape[-1]
    groups = width // lanes
    subs = send_hbm.shape[0] // WIN
    halo = upper_ref.shape[0]
    ints = started([(owner_hbm, owner_ref), (halo_hbm, halo_ref)], int_sems)
    parts = [pl.ds(at, blocks // PARTS) for at in range(0, blocks, blocks // PARTS)]
    loads = started([(nodes_hbm.at[part], nodes_ref.at[part]) for part in parts], node_sems)
    held = started(
        [
            (first_hbm, first_ref),
            (tiles_hbm, tiles_ref),
            (bias_hbm, bias_ref.at[0]),
            (gain_hbm, gain_ref.at[0]),
        ],
        held_sems,
    )
    few = blocks // PARTS
    row = lax.broadcasted_iota(jnp.int32, (few * tile, few * rows), 0)
    col = lax.broadcasted_iota(jnp.int32, (few * tile, few * rows), 1)
    average = jnp.where(col // POOL == row, 1.0 / POOL, 0.0).astype(BF16)
    for copy in ints:
        copy.wait()
    slots = owner_slots(owner_ref, count_ref, blocks)
    for k, (d, r) in enumerate(slots):
        index_ref[d * 2 + r] = k
        slot_ref[k] = jnp.full(slot_ref.shape[1:], (d * 2 + r) * tile, jnp.int32)
    lane = lax.broadcasted_iota(jnp.int32, (tile, lanes), 1)
    for d in range(WIN):
        tag = jnp.where((lane // tile) % 2 == 0, index_ref[2 * d], index_ref[2 * d + 1])
        tag = tag.astype(F32).astype(BF16)
        send_ref[d, groups * 2] = tag
    outs = []
    for part, load in enumerate(loads):
        load.wait()
        if part == PARTS - 1:
            outs += started([(nodes_ref.at[halo_ref[h]], lower_hbm.at[h]) for h in range(halo)], lower_sems)
        nodes = nodes_ref[part * few : (part + 1) * few].reshape(few * rows, width)
        pooled = jnp.dot(average, nodes, preferred_element_type=F32).astype(BF16)
        for k, (d, r) in enumerate(slots[part * few : (part + 1) * few]):
            for c in range(groups):
                piece = pooled[k * tile : (k + 1) * tile, c * lanes : (c + 1) * lanes]
                send_ref[d, c * 2 + r] = piece
    outs += started(
        [(send_ref.at[d], send_hbm.at[d * subs + s]) for d in range(WIN) for s in range(subs)], send_sems
    )
    for h in range(halo):
        upper_ref[h] = nodes_ref[halo_ref[halo + h]]
    for copy in held + outs:
        copy.wait()


def pack(pool_owner, halo_blocks, blocks, first, tiles, bias, gain, subs):
    count, rows, width = blocks.shape
    tile = rows // POOL
    halos = halo_blocks.shape[0]
    lanes = 128
    pieces = 2 * (width // lanes) + 1
    return pl.pallas_call(
        pack_kernel,
        name="pack",
        out_shape=(
            jax.ShapeDtypeStruct((WIN * subs, pieces, tile, lanes), BF16),
            jax.ShapeDtypeStruct((halos // 2, rows, width), BF16),
            jax.ShapeDtypeStruct((halos // 2, rows, width), BF16),
            jax.ShapeDtypeStruct((count, 8, rows), jnp.int32),
            jax.ShapeDtypeStruct(first.shape, BF16),
            jax.ShapeDtypeStruct(tiles.shape, BF16),
            jax.ShapeDtypeStruct((1, width), F32),
            jax.ShapeDtypeStruct((1, width), F32),
        ),
        in_specs=[HBM_SPEC] * 7,
        out_specs=(ANY_SPEC,) * 2 + (VMEM_SPEC,) * 6,
        scratch_shapes=[
            pltpu.SMEM((count,), jnp.int32),
            pltpu.SMEM((halos,), jnp.int32),
            pltpu.VMEM(blocks.shape, BF16),
            pltpu.VMEM((WIN, pieces, tile, lanes), BF16),
            pltpu.SMEM((WIN,), jnp.int32),
            pltpu.SMEM((2 * WIN,), jnp.int32),
            pltpu.SemaphoreType.DMA((2,)),
            pltpu.SemaphoreType.DMA((PARTS,)),
            pltpu.SemaphoreType.DMA((4,)),
            pltpu.SemaphoreType.DMA((halos // 2,)),
            pltpu.SemaphoreType.DMA((WIN * subs,)),
        ],
        compiler_params=PARAMS,
        cost_estimate=pl.CostEstimate(flops=1 << 27, bytes_accessed=3 << 20, transcendentals=0),
    )(*held_in_hbm(pool_owner, halo_blocks, blocks, first, tiles, bias, gain))


def normalised(values, gain):
    row_mean = jnp.mean(values, axis=-1, keepdims=True)
    centred = values - row_mean
    variance = jnp.mean(centred * centred, axis=-1, keepdims=True)
    return centred * lax.rsqrt(variance + 1e-05) * gain


def network(nodes, messages, first_ref, bias_ref, second_ref, gain_ref):
    width = nodes.shape[1]
    hidden = jnp.dot(nodes, first_ref[:width], preferred_element_type=F32)
    hidden += jnp.dot(messages, first_ref[width:], preferred_element_type=F32)
    hidden = jnp.maximum(hidden + bias_ref[...], 0.0).astype(BF16)
    projected = jnp.dot(hidden, second_ref[...], preferred_element_type=F32)
    return normalised(projected, gain_ref[...])


def coarse_kernel(
    sub_ref, offset_hbm, second_hbm, arrived_ref, first_ref, tiles_ref, bias_ref, gain_ref, reply_ref,
    offset_ref, second_ref, sems,
):
    senders, pieces, tile, lanes = arrived_ref.shape
    groups = pieces // 2
    subs = senders // WIN
    entries, rows, _ = tiles_ref.shape
    loads = started([(offset_hbm, offset_ref), (second_hbm, second_ref)], sems)
    row = lax.broadcasted_iota(jnp.int32, (rows, rows), 0)
    col = lax.broadcasted_iota(jnp.int32, (rows, rows), 1)
    same_row = row % tile == col % tile

    def arrived_rows(s):
        return jnp.concatenate(
            [
                jnp.concatenate([arrived_ref[m * subs + s, c * 2 + r] for c in range(groups)], axis=1)
                for m in range(WIN)
                for r in range(2)
            ],
            axis=0,
        )

    def placing(s):
        tags = jnp.zeros((8, lanes), F32)
        lane = lax.broadcasted_iota(jnp.int32, (8, lanes), 1)
        for m in range(WIN):
            tag = arrived_ref[m * subs + s, groups * 2].astype(F32)[:8]
            tags = jnp.where(lane // (2 * tile) == m, tag, tags)
        return jnp.where(same_row & (row // tile == tags[:1].astype(jnp.int32)), 1.0, 0.0)

    own = sub_ref[0]
    own_rows = arrived_rows(own)
    own_back = placing(own).T.astype(BF16)
    loads[0].wait()
    weights, sources = [], []
    for e in range(entries):
        s = lax.rem(own + offset_ref[e], subs)
        sources.append(arrived_rows(s))
        by_col = jnp.dot(tiles_ref[e], placing(s).astype(BF16), preferred_element_type=F32)
        weights.append(by_col.astype(BF16))
    by_col = jnp.concatenate(weights, axis=1)
    by_both = jnp.dot(own_back, by_col, preferred_element_type=F32).astype(BF16)
    messages = jnp.dot(by_both, jnp.concatenate(sources, axis=0), preferred_element_type=F32)
    loads[1].wait()
    delta = network(own_rows, messages.astype(BF16), first_ref, bias_ref, second_ref, gain_ref)
    delta = delta.astype(BF16)
    for m in range(WIN):
        for r in range(2):
            at = (m * 2 + r) * tile
            reply_ref[m, r] = delta[at : at + tile]


def coarse_update(own_sub, offsets, second, arrived, held):
    return pl.pallas_call(
        coarse_kernel,
        name="coarse",
        out_shape=jax.ShapeDtypeStruct((WIN, 2, arrived.shape[2], second.shape[0]), BF16),
        in_specs=[SMEM_SPEC, HBM_SPEC, HBM_SPEC] + [VMEM_SPEC] * 5,
        out_specs=VMEM_SPEC,
        scratch_shapes=[
            pltpu.SMEM(offsets.shape, jnp.int32),
            pltpu.VMEM(second.shape, BF16),
            pltpu.SemaphoreType.DMA((2,)),
        ],
        compiler_params=PARAMS,
        cost_estimate=pl.CostEstimate(flops=1 << 29, bytes_accessed=3 << 20, transcendentals=0),
    )(own_sub, *held_in_hbm(offsets, second), arrived, *held)


def add_messages(
    target_ref, source_ref, live, table, tiles, total, order, place, loads
):
    blocks = total.shape[0]
    entries = target_ref.shape[0]
    slots = order.shape[0]
    for b in range(blocks + 1):
        place[b] = 0
    for i in range(slots):
        order[i] = entries
    bins = []
    for e in range(entries):
        b = jnp.where(e < live, target_ref[e], blocks)
        place[b] = place[b] + 1
        bins.append(b)
    at = 0
    for b in range(blocks):
        steps = (place[b] + (DEPTH - 1)) // DEPTH
        place[b] = at * DEPTH
        at = at + steps
    place[blocks] = slots - entries
    used = at
    for e in range(entries):
        at = place[bins[e]]
        place[bins[e]] = at + 1
        order[at] = e + (source_ref[e] << 8) + (bins[e] << 16)
    for copy in loads:
        copy.wait()

    @pl.loop(0, (used + (SIDE - 1)) // SIDE)
    def _(i):
        products = []
        for u in range(SIDE):
            codes = [order[(i * SIDE + u) * DEPTH + g] for g in range(DEPTH)]
            left = jnp.concatenate([tiles[code & 255] for code in codes], axis=1)
            right = jnp.concatenate([table[(code >> 8) & 255] for code in codes], axis=0)
            product = jnp.dot(left, right, preferred_element_type=F32)
            products.append((codes[0] >> 16, product))
        for b, product in products:
            total[b] += product


def order_slots(entries, blocks):
    groups = entries // DEPTH + blocks
    return (groups + SIDE - 1) // SIDE * SIDE * DEPTH + entries


def fine_body(
    target_hbm, source_hbm, count_ref, lower_hbm, upper_hbm, edges_hbm, nodes_hbm,
    first_hbm, bias_hbm, second_hbm, gain_hbm,
    target_ref, source_ref, table, tiles, total, order, place,
    first_ref, bias_ref, second_ref, gain_ref, sems, use,
):
    entries = edges_hbm.shape[0]
    halo = lower_hbm.shape[0]
    blocks, rows, width = total.shape
    loads = started(
        [
            (target_hbm, target_ref),
            (source_hbm, source_ref),
            (edges_hbm, tiles.at[pl.ds(0, entries)]),
            (nodes_hbm, table.at[pl.ds(0, blocks)]),
            (lower_hbm, table.at[pl.ds(blocks, halo)]),
            (upper_hbm, table.at[pl.ds(blocks + halo, halo)]),
            (first_hbm, first_ref),
            (second_hbm, second_ref),
            (bias_hbm, bias_ref.at[0]),
            (gain_hbm, gain_ref.at[0]),
        ],
        sems,
    )
    tiles[entries] = jnp.zeros(tiles.shape[1:], BF16)
    total[...] = jnp.zeros_like(total)
    for copy in loads[:2]:
        copy.wait()
    add_messages(target_ref, source_ref, count_ref[0], table, tiles, total, order, place, loads[2:6])
    for copy in loads[6:]:
        copy.wait()
    for i in range(blocks // 2):
        nodes = table[2 * i : 2 * i + 2].reshape(2 * rows, width)
        messages = total[2 * i : 2 * i + 2].reshape(2 * rows, width).astype(BF16)
        use(i, nodes.astype(F32) + network(nodes, messages, first_ref, bias_ref, second_ref, gain_ref))


def fine_scratch(edges, nodes, halo, first, second):
    entries, rows, _ = edges.shape
    blocks, _, width = nodes.shape
    return [
        pltpu.SMEM((entries,), jnp.int32),
        pltpu.SMEM((entries,), jnp.int32),
        pltpu.VMEM((blocks + 2 * halo, rows, width), BF16),
        pltpu.VMEM((entries + 1, rows, rows), BF16),
        pltpu.VMEM(nodes.shape, F32),
        pltpu.SMEM((order_slots(entries, blocks),), jnp.int32),
        pltpu.SMEM((blocks + 1,), jnp.int32),
        pltpu.VMEM(first.shape, BF16),
        pltpu.VMEM((1, width), F32),
        pltpu.VMEM(second.shape, BF16),
        pltpu.VMEM((1, width), F32),
        pltpu.SemaphoreType.DMA((10,)),
    ]


FINE_SPECS = [HBM_SPEC, HBM_SPEC, SMEM_SPEC, ANY_SPEC, ANY_SPEC] + [HBM_SPEC] * 6


def fine_inputs(entries, lower, upper, edges, nodes, first, bias, second, gain):
    target, source, count = entries
    return [
        *held_in_hbm(target, source),
        count,
        lower,
        upper,
        *held_in_hbm(edges, nodes, first, bias, second, gain),
    ]


def fine_kernel(late_ref, *refs):
    fine_in, partial_ref, fine_refs = refs[:11], refs[11], refs[12:]
    _, rows, width = partial_ref.shape

    def use(i, values):
        partial_ref[2 * i : 2 * i + 2] = values.astype(BF16).reshape(2, rows, width)

    @pl.when(late_ref[0] == 0)
    def _():
        fine_body(*fine_in, *fine_refs, use)


def fine_update(late, fine_in):
    edges, nodes, first, _, second, _ = fine_in[5:]
    return pl.pallas_call(
        fine_kernel,
        name="fine",
        out_shape=jax.ShapeDtypeStruct(nodes.shape, BF16),
        in_specs=[SMEM_SPEC] + FINE_SPECS,
        out_specs=VMEM_SPEC,
        scratch_shapes=fine_scratch(edges, nodes, fine_in[3].shape[0], first, second),
        compiler_params=PARAMS,
        cost_estimate=pl.CostEstimate(flops=1 << 37, bytes_accessed=1 << 20, transcendentals=0),
    )(late, *fine_in)


def finish_kernel(late_ref, mem_ref, partial_ref, slot_ref, replies_ref, *refs):
    fine_in, out_hbm, (*fine_refs, out_ref, out_sems) = refs[:11], refs[11], refs[12:]
    blocks, rows, width = partial_ref.shape
    row = lax.broadcasted_iota(jnp.int32, (rows, rows), 0)
    col = lax.broadcasted_iota(jnp.int32, (rows, rows), 1)
    place = col - row // POOL
    mine = [replies_ref[q, mem_ref[0]].reshape(rows // WIN, width) for q in range(WIN)]
    reply = jnp.concatenate(mine, axis=0)

    def use(i, values):
        at = pl.ds(2 * i, 2)
        spread = [jnp.where(place == slot_ref[k][:1], 1.0, 0.0) for k in (2 * i, 2 * i + 1)]
        spread = jnp.concatenate(spread, axis=0).astype(BF16)
        back = jnp.dot(spread, reply, preferred_element_type=F32)
        out_ref[2 * i : 2 * i + 2] = (values + back).astype(BF16).reshape(2, rows, width)
        started([(out_ref.at[at], out_hbm.at[at])], out_sems.at[pl.ds(i, 1)])

    @pl.when(late_ref[0] == 0)
    def _():
        for i in range(blocks // 2):
            use(i, partial_ref[2 * i : 2 * i + 2].reshape(2 * rows, width).astype(F32))

    @pl.when(late_ref[0] == 1)
    def _():
        fine_body(*fine_in, *fine_refs, use)

    for i in range(blocks // 2):
        at = pl.ds(2 * i, 2)
        pltpu.make_async_copy(out_ref.at[at], out_hbm.at[at], out_sems.at[i]).wait()


def finish(late, own_mem, partial, slots, replies, fine_in):
    edges, nodes, first, _, second, _ = fine_in[5:]
    return pl.pallas_call(
        finish_kernel,
        name="finish",
        out_shape=jax.ShapeDtypeStruct(partial.shape, BF16),
        in_specs=[SMEM_SPEC] * 2 + [VMEM_SPEC] * 3 + FINE_SPECS,
        out_specs=ANY_SPEC,
        scratch_shapes=fine_scratch(edges, nodes, fine_in[3].shape[0], first, second)
        + [pltpu.VMEM(partial.shape, BF16), pltpu.SemaphoreType.DMA((partial.shape[0] // 2,))],
        compiler_params=PARAMS,
        cost_estimate=pl.CostEstimate(flops=1 << 25, bytes_accessed=4 << 20, transcendentals=0),
    )(late, own_mem, partial, slots, replies, *fine_in)


def per_device(
    fine_nodes,
    edge_tiles,
    edge_target,
    edge_source,
    edge_count,
    halo_blocks,
    pool_owner,
    coarse_tiles,
    pooled_block_source_index,
    fine_first,
    fine_bias,
    fine_second,
    fine_gain,
    coarse_first,
    coarse_bias,
    coarse_second,
    pooled_level_scale_factor,
):
    block_count = pool_owner.shape[0]
    rows = edge_tiles.shape[1]
    width = fine_nodes.shape[1]
    subs = lax.axis_size("sub")
    everyone = ("win", "mem", "sub")
    devices = lax.axis_size(everyone)
    blocks = fine_nodes.reshape(block_count, rows, width)

    own_sub = lax.axis_index("sub").astype(jnp.int32)[None]
    index = lax.axis_index(everyone)
    late = ((index % ROW == ROW - 1) & (index < devices - 1)).astype(jnp.int32)[None]
    send, lower, upper, slots, *held = pack(
        pool_owner,
        halo_blocks,
        blocks,
        coarse_first,
        coarse_tiles,
        coarse_bias,
        pooled_level_scale_factor,
        subs,
    )
    from_lower = lax.ppermute(upper, everyone, [(i, i + 1) for i in range(devices - 1)])
    from_upper = lax.ppermute(
        lower, everyone, [(i + 1, i) for i in range(devices - 1) if (i + 1) % ROW]
    )
    arrived = lax.all_to_all(send, ("mem", "sub"), 0, 0, tiled=True)
    entries = (edge_target, edge_source, edge_count)
    network_in = (edge_tiles, blocks, fine_first, fine_bias, fine_second, fine_gain)
    partial = fine_update(late, fine_inputs(entries, from_lower, from_upper, *network_in))
    lower, partial = lax.optimization_barrier((lower, partial))
    late_upper = lax.ppermute(lower, everyone, [(i, i - 1) for i in range(ROW, devices, ROW)])
    reply = coarse_update(own_sub, pooled_block_source_index, coarse_second, arrived, held)
    replies = lax.all_gather(reply, "mem")
    own_mem = lax.axis_index("mem").astype(jnp.int32)[None]
    late_in = fine_inputs(entries, from_lower, late_upper, *network_in)
    return finish(late, own_mem, partial, slots, replies, late_in).reshape(fine_nodes.shape)


def solution(mesh):
    dom, sub = mesh.devices.shape
    split = Mesh(mesh.devices.reshape(dom // WIN, WIN, sub), ("win", "mem", "sub"))
    every = ("win", "mem", "sub")
    placed = (
        P(every, None),
        P(every, None, None),
        P(every),
        P(every),
        P(every),
        P(every),
        P(every),
        P(every, None, None),
        P(every),
        P(),
        P(),
        P(),
        P(),
        P(),
        P(),
        P(),
        P(),
    )
    return jax.shard_map(
        per_device, mesh=split, in_specs=placed, out_specs=P(every, None), check_vma=False
    )
```
